512 devices in a mesh: slab: 128 (over z_lo, x, y, core), pencil: 4 (over z_hi).
Axes of the slice: x: 4, y: 8, z: 8 (z_hi: 4, z_lo: 2; z = z_hi * 2 + z_lo), core: 2. Of those that a mesh axis runs over, the one named last changes fastest.
Arguments:
- density: float32 [256, 256, 256], P('slab', 'pencil'), may hold values from -6 to 6
- weight_down: bfloat16 [48, 24], replicated, may hold values from -1.25 to 1.25
- bias_down: float32 [48], replicated, may hold values from -3 to 3
- weight_conv: bfloat16 [27, 48, 48], replicated, may hold values from -0.15625 to 0.15625
- bias_conv: float32 [48], replicated, may hold values from -3 to 3
- weight_out: bfloat16 [3, 48], replicated, may hold values from -0.875 to 0.875
- observed: float32 [3, 128, 128, 128], P(None, 'slab', 'pencil'), may hold values from -6 to 6
- noise_precision: float32 [128, 128, 128], P('slab', 'pencil'), may hold values from 0.25 to 4
Outputs:
- gradient: float32 [256, 256, 256], P('slab', 'pencil')
The draws below stay inside these ranges and needn't reach their ends.
All inputs are finite; a program needn't handle non-finite values.
Results may differ from the reference program's by a relative error of at most 0.0033.
Values may be sent and summed in bfloat16 or wider, within the bound.
A program may use at most 128 MiB of HBM per device.

```python
import math
import jax
import jax.numpy as jnp
from jax import lax

GY = 256
GZ = 256
CH = 48
GX = 256


def shard_levels(rng, shape, pieces, least, largest):
    def one(dim, shards_of):
        draws = jax.random.uniform(jax.random.fold_in(jax.random.fold_in(rng, 6), dim), (shards_of,), jnp.float32, least / len(pieces), largest / len(pieces))
        return jnp.repeat(jnp.exp(draws), shape[dim] // shards_of).reshape((-1,) + (1,) * (len(shape) - dim - 1))

    factor_of = one(*pieces[0])
    for cut in pieces[1:]:
        factor_of = factor_of * one(*cut)
    return factor_of


def scatter_about(key, dims, spread, most, split=(), kind=jnp.bfloat16):
    array = jax.random.normal(key, dims, jnp.float32) * spread
    if len(split) > 0:
        array = shard_levels(key, dims, split, -0.22, 0.18) * array
    return jnp.clip(array, min=-most, max=most).astype(kind)


def setup_inputs(seed: int = 0) -> dict:
    key_list = jax.random.split(jax.random.key(seed), 9)
    return {
        "density": scatter_about(key_list[0], (GX, GY, GZ), 1.0, 6.0, ((0, 128), (1, 4)), jnp.float32),
        "weight_down": scatter_about(key_list[1], (CH, 24), 24 ** -0.5, 1.25),
        "bias_down": scatter_about(key_list[2], (CH,), 0.5, 3.0, (), jnp.float32),
        "weight_conv": scatter_about(key_list[3], (27, CH, CH), (27 * CH) ** -0.5, 0.15625),
        "bias_conv": scatter_about(key_list[4], (CH,), 0.5, 3.0, (), jnp.float32),
        "weight_out": scatter_about(key_list[5], (3, CH), CH ** -0.5, 0.875),
        "observed": scatter_about(key_list[6], (3, GX // 2, GY // 2, GZ // 2), 1.0, 6.0, ((1, 128), (2, 4)), jnp.float32),
        "noise_precision": jnp.clip(jnp.exp(math.log(4.0) - 2.7725887 * jax.random.uniform(key_list[7], (GX // 2, GY // 2, GZ // 2), jnp.float32) ** shard_levels(key_list[7], (GX // 2, GY // 2, GZ // 2), ((0, 128), (1, 4)), -0.2, 0.2)), 0.25, 4.0),
    }


growth_factor = 3.0
highest = lax.Precision.HIGHEST


def wave_axis(length, count, offset):
    indices = offset + jnp.arange(count, dtype=jnp.int32)
    signed = jnp.where(indices < length // 2, indices, indices - length)
    numerator = jnp.where(indices == length // 2, 0, signed)
    spacing = 2.0 * math.pi / length
    return indices, numerator.astype(jnp.float32) * spacing, signed.astype(jnp.float32) * spacing


def mode_factors(half_z):
    index_x, along_x, full_x = wave_axis(GX, GX, 0)
    index_y, along_y, full_y = wave_axis(GY, GY, 0)
    index_z, along_z, full_z = wave_axis(GZ, half_z, 0)
    square = (full_x * full_x)[:, None, None] + (full_y * full_y)[None, :, None] + (full_z * full_z)[None, None, :]
    anchor = (index_x[:, None, None] == 0) & (index_y[None, :, None] == 0) & (index_z[None, None, :] == 0)
    square = square + anchor.astype(jnp.float32)
    extent = square.shape
    numerators = jnp.stack([
        jnp.broadcast_to(along_x[:, None, None], extent),
        jnp.broadcast_to(along_y[None, :, None], extent),
        jnp.broadcast_to(along_z[None, None, :], extent)])
    return growth_factor * numerators / square[None]


def to_cells(modes):
    planes_xy = jnp.fft.ifft2(modes, axes=(-3, -2)) * (GX * GY)
    padded = jnp.concatenate([planes_xy, jnp.zeros_like(planes_xy)], axis=-1)
    return jnp.real(jnp.fft.ifft(padded, axis=-1)) * GZ


def gate_slope(values):
    sigmoid = jax.nn.sigmoid(values)
    return sigmoid * (1.0 + values * (1.0 - sigmoid))


def periodic_conv(values, weights):
    padded = jnp.pad(values.astype(jnp.float32), ((0, 0), (1, 1), (1, 1), (1, 1)), mode='wrap')
    outputs = weights.shape[1]
    inputs = weights.shape[2]
    kernel = weights.astype(jnp.float32).reshape(3, 3, 3, outputs, inputs).transpose(3, 4, 0, 1, 2)
    result = lax.conv_general_dilated(padded[None], kernel, (1, 1, 1), 'VALID',
                                      dimension_numbers=('NCDHW', 'OIDHW', 'NCDHW'), precision=highest)
    return result[0]


def reference(density, weight_down, bias_down, weight_conv, bias_conv, weight_out, observed, noise_precision):
    half_z = GZ // 2
    cells_total = GX * GY * GZ
    doubled = jnp.where(jnp.arange(half_z, dtype=jnp.int32) == 0, 1.0, 2.0).astype(jnp.float32)
    factors = mode_factors(half_z)
    modes = jnp.fft.fft2(jnp.fft.rfft(density, axis=2)[:, :, :half_z], axes=(0, 1))
    displaced_hat = 1j * factors * modes[None]
    displaced = (to_cells(displaced_hat * doubled) / cells_total).astype(jnp.bfloat16)
    kernel_down = weight_down.astype(jnp.float32).reshape(CH, 3, 2, 2, 2)
    grouped = displaced.astype(jnp.float32).reshape(3, GX // 2, 2, GY // 2, 2, half_z, 2)
    pre_down = jnp.einsum('oiabc,ixaybzc->oxyz', kernel_down, grouped, precision=highest) + bias_down[:, None, None, None]
    framed = jax.nn.silu(pre_down).astype(jnp.bfloat16)
    pre_conv = periodic_conv(framed, weight_conv) + bias_conv[:, None, None, None]
    hidden = jax.nn.silu(pre_conv).astype(jnp.bfloat16)
    predicted = jnp.einsum('jo,oxyz->jxyz', weight_out.astype(jnp.float32), hidden.astype(jnp.float32), precision=highest)
    residual = noise_precision[None] * (predicted - observed)
    grad_hidden = jnp.einsum('jo,jxyz->oxyz', weight_out.astype(jnp.float32), residual, precision=highest)
    grad_conv = (grad_hidden * gate_slope(pre_conv)).astype(jnp.bfloat16)
    flipped = jnp.swapaxes(weight_conv[::-1], 1, 2)
    grad_down = (periodic_conv(grad_conv, flipped) * gate_slope(pre_down)).astype(jnp.bfloat16)
    grad_fine = jnp.einsum('oiabc,oxyz->ixaybzc', kernel_down, grad_down.astype(jnp.float32),
                           precision=highest).reshape(3, GX, GY, GZ)
    grad_modes = jnp.fft.fft2(jnp.fft.rfft(grad_fine, axis=3)[..., :half_z] * (doubled / cells_total), axes=(1, 2))
    combined = jnp.sum(-1j * factors * grad_modes, axis=0)
    return to_cells(combined).astype(jnp.float32)
```

```python
import functools

import jax
import jax.numpy as jnp
import ml_dtypes
import numpy as np
from jax import lax
from jax.experimental import pallas as pl
from jax.experimental.pallas import tpu as pltpu
from jax.sharding import PartitionSpec as P

MESH = pl.DeviceIdType.MESH
BF = jnp.bfloat16
F32 = jnp.float32
N = 256
GROWTH = 3.0
TWO_PI = 2.0 * np.pi
KINDS = (F32, F32, F32, F32, BF, F32, F32, F32)


def theta(a, b):
    return TWO_PI * ((a[:, None].astype(np.int64) * b[None, :]) % N) / N


def grid(*sizes):
    return [g.reshape(-1) for g in np.meshgrid(*[np.arange(s) for s in sizes], indexing="ij")]


def signed(k):
    return np.where(k < N // 2, k, k - N)


def wave(k):
    return np.where(k == N // 2, 0, signed(k)) * (TWO_PI / N)


def complex_rows(angle, c_out, c_in, sign, turn):
    value = np.exp(1j * sign * angle) * (1j**turn)
    a, b = c_out[:, None], c_in[None, :]
    same = a == b
    cross = np.where((a == 0) & (b == 1), -value.imag, value.imag)
    return np.where(same, value.real, cross)


def swap_rows(order_in, order_out, sign):
    rows_in = {key: i for i, key in enumerate(order_in)}
    count = len(order_in)
    out = np.zeros((2 * count, count))
    for i, key in enumerate(order_out):
        out[i, rows_in[key]] = 1.0
        name = dict(key)
        name["c"] = 1 - name["c"]
        other = tuple(name.items())
        out[count + i, rows_in[other]] = (1.0 if dict(key)["c"] == 0 else -1.0) * (-sign)
    return out


def keys(spec, canon):
    names = [n for n, _ in spec]
    axes = grid(*[s for _, s in spec])
    out = []
    for values in zip(*axes):
        d = dict(zip(names, (int(v) for v in values)))
        out.append(tuple((n, d[n]) for n in canon))
    return out


def tables():
    t = {}
    half = np.where(np.arange(N // 2) == 0, 1.0, 2.0) / float(N) ** 3
    z = np.arange(N)
    q, c, k = grid(16, 2, 8)
    kz = 8 * q + k
    t["zf"] = complex_rows(theta(kz, z), c, np.zeros(N, np.int64), -1, 0)
    par, zz = grid(2, 128)
    zc = 2 * zz + par
    back = complex_rows(theta(kz, zc), c, np.zeros(N, np.int64), -1, 0) * half[kz][:, None]
    t["zb"] = np.stack([back, back * wave(kz)[:, None]])
    q, k, c = grid(16, 8, 2)
    kz = 8 * q + k
    inv = complex_rows(theta(kz, zc).T, np.zeros(N, np.int64), c, 1, 0).T * half[kz][:, None]
    t["zi"] = np.stack([inv, inv * wave(kz)[:, None]])
    t["zj"] = complex_rows(theta(kz, z).T, np.zeros(N, np.int64), c, 1, 0).T
    a = np.arange(N)
    base = np.concatenate([np.cos(theta(a, a)), np.sin(theta(a, a))], axis=0)
    qy = wave(a)
    t["yt"] = base
    times = np.concatenate([qy, qy])[:, None] * base
    t["yi"] = np.concatenate([times, base], axis=1)
    by = base * qy[None, :]
    t["yb"] = np.concatenate([by, base], axis=0)
    x1, c_out, kx = grid(2, 2, N)
    r, w, c_in = grid(32, 4, 2)
    pos = lambda x1: 128 * (w // 2) + 4 * r + 2 * (w % 2) + x1
    full = [complex_rows(theta(kx[:512], pos(v)), c_out[:512], c_in, -1, 0) for v in (0, 1)]
    t["xf"] = np.concatenate(full, axis=0)
    c_k, kx = grid(2, N)
    t["xj"] = np.concatenate(
        [complex_rows(theta(kx, pos(v)).T, c_in, c_k, 1, -1) for v in (0, 1)], axis=0
    )
    r, c, x8 = grid(32, 2, 8)
    t["xi"] = complex_rows(theta(kx, 8 * r + x8).T, c, c_k, 1, 1)
    r, x8, c = grid(32, 8, 2)
    t["xb"] = complex_rows(theta(kx, 8 * r + x8), c_k, c, -1, 0)
    pairs = {}
    for name, value in t.items():
        high = value.astype(np.float32).astype(ml_dtypes.bfloat16)
        low = (value - high.astype(np.float64)).astype(np.float32).astype(ml_dtypes.bfloat16)
        pairs[name] = np.stack([high, low])
    canon = ("w", "c", "k")
    s = {}
    s["pf"] = swap_rows(
        keys((("w", 4), ("c", 2), ("k", 8)), canon), keys((("k", 8), ("w", 4), ("c", 2)), canon), -1
    )
    s["pj"] = swap_rows(
        keys((("k", 8), ("w", 4), ("c", 2)), canon), keys((("w", 4), ("k", 8), ("c", 2)), canon), 1
    )
    s["pi"] = swap_rows(
        keys((("k", 8), ("c", 2), ("w", 8)), canon), keys((("w", 8), ("k", 8), ("c", 2)), canon), 1
    )
    s["pb"] = swap_rows(
        keys((("w", 8), ("c", 2), ("k", 8)), canon), keys((("k", 8), ("w", 8), ("c", 2)), canon), -1
    )
    par, i, a, y = grid(2, 3, 2, 16)
    e2 = np.zeros((192, 24))
    e2[np.arange(192), 8 * i + 4 * a + 2 * (y % 2) + par] = 1.0
    s["e2t"] = e2
    e1 = np.zeros((384, 48))
    e1[np.arange(384), np.arange(384) % 48] = 1.0
    s["e1"] = e1
    for name, value in s.items():
        pairs[name] = value.astype(np.float32).astype(ml_dtypes.bfloat16)
    return pairs


def dot(a, b, ca, cb):
    return lax.dot_general(a, b, (((ca,), (cb,)), ((), ())), preferred_element_type=F32)


def nn(a, b):
    return dot(a, b, 1, 0)


def nt(a, b):
    return dot(a, b, 1, 1)


def tn(a, b):
    return dot(a, b, 0, 0)


def roll(x, shift):
    return pltpu.roll(x, shift % x.shape[-1], x.ndim - 1)


def split(x):
    high = x.astype(BF)
    return high, (x - high.astype(F32)).astype(BF)


def lanes():
    return lax.broadcasted_iota(jnp.int32, (1, 128), 1)


def low_halves(a, b):
    return jnp.where(lanes() < 64, a, roll(b, 64))


def high_halves(a, b):
    return jnp.where(lanes() < 64, roll(a, 64), b)


def transpose_groups(tiles):
    tiles = list(tiles)
    for d in (1, 2, 4):
        odd = (lanes() // (16 * d)) % 2 == 1
        for i in range(8):
            if i & d:
                continue
            low, high = tiles[i], tiles[i + d]
            tiles[i] = jnp.where(odd, roll(high, 16 * d), low)
            tiles[i + d] = jnp.where(odd, high, roll(low, 128 - 16 * d))
    return tiles


def cat(parts, axis):
    return jnp.concatenate(list(parts), axis=axis)


def parts_of(x, kind):
    return (x.astype(BF),) if kind == BF else split(x)


def pair_swapped(moved, rows, fields):
    return [
        cat([moved[:rows, 256 * f : 256 * f + 256], moved[rows:, 256 * f : 256 * f + 256]], 1)
        for f in range(fields)
    ]


def table_left(form, t, x, index=()):
    high, low = t[(0, *index)], t[(1, *index)]
    out = form(high, x[0]) + form(low, x[0])
    if len(x) > 1:
        out = out + form(high, x[1])
    return out


def table_right(form, x, t, index=()):
    high, low = t[(0, *index)], t[(1, *index)]
    out = form(x[0], high) + form(x[0], low)
    if len(x) > 1:
        out = out + form(x[1], high)
    return out


def stage_z_forward(t, density):
    return table_left(nt, t["zf"], split(density)).reshape(16, 16, 128)


def stage_y_forward(t, got):
    z_rows = [got[4 * i : 4 * i + 4].reshape(64, 128).astype(F32) for i in range(4)]
    x = cat(
        [f(z_rows[2 * a], z_rows[2 * a + 1]) for f in (low_halves, high_halves) for a in (0, 1)], 1
    )
    left = [
        cat(pair_swapped(nn(t["pf"][...], part).astype(BF), 64, 2), 0)
        for part in parts_of(x, got.dtype)
    ]
    out = table_right(nn, left, t["yt"])
    first, second = out[:64], out[64:]
    parts = []
    for a in (0, 1):
        u, v = first[:, 128 * a : 128 * a + 128], second[:, 128 * a : 128 * a + 128]
        parts += [low_halves(u, v), high_halves(u, v)]
    return jnp.stack([p.reshape(8, 8, 128) for p in parts], axis=1).reshape(32, 8, 128)


def factors(q, r):
    kz = 8 * q + r // 4
    row = lax.broadcasted_iota(jnp.int32, (N, 128), 0)
    lane = lax.broadcasted_iota(jnp.int32, (N, 128), 1)
    ky = 64 * (r % 4) + lane % 64
    spacing = F32(TWO_PI / N)

    def full(k):
        return jnp.where(k < N // 2, k, k - N).astype(F32) * spacing

    fx, fy = full(row), full(ky)
    fz = (kz + 0 * row).astype(F32) * spacing
    square = fx * fx + fy * fy + fz * fz
    anchor = (row == 0) & (ky == 0) & (kz == 0)
    square = jnp.where(anchor, F32(1.0), square)
    qx = jnp.where(row == N // 2, F32(0.0), fx)
    first = lane < 64
    inverse = F32(GROWTH) / square
    return inverse, jnp.where(first, inverse, inverse * qx), jnp.where(first, qx, F32(1.0))


def times_rows(x, factor):
    return (x.reshape(2, N, 128) * factor[None]).reshape(2 * N, 128)


def stage_x_forward(t, got, factor):
    y = table_left(nn, t["xf"], split(got.reshape(256, 128)))
    z = jnp.where(lanes() < 64, y[:512], y[512:])
    modes = times_rows(z + roll(z, 64), factor)
    return table_left(nn, t["xi"], split(modes)).reshape(32, 16, 128)


def stage_y_inverse(t, got):
    kind = got.dtype
    got = got.reshape(8, 4, 16, 128)
    tile = [got[:, i].reshape(128, 128).astype(F32) for i in range(4)]
    x = cat([f(tile[2 * a], tile[2 * a + 1]) for f in (low_halves, high_halves) for a in (0, 1)], 1)
    left = [
        pair_swapped(nn(t["pi"][...], part).astype(BF), 128, 2) for part in parts_of(x, kind)
    ]
    ox = table_right(nn, [p[1] for p in left], t["yt"])
    oyz = table_right(nn, [p[0] for p in left], t["yi"])
    fields = (ox, oyz[:, :256], oyz[:, 256:])
    tiles = [
        cat([f[16 * i : 16 * i + 16, 128 * h : 128 * h + 128] for f in fields for h in (0, 1)], 0)
        for i in range(8)
    ]
    tiles = transpose_groups(tiles)
    return jnp.stack(
        [tiles[i].reshape(3, 2, 16, 128)[:, h] for h in (0, 1) for i in range(8)], axis=0
    )


def stage_z_inverse(t, got):
    psi = []
    for i in range(3):
        m = got[:, i].reshape(256, 128)
        psi.append(
            table_right(tn, parts_of(m, got.dtype), t["zi"], (1 if i == 2 else 0,)).astype(BF)
        )
    rows = []
    for par in (0, 1):
        for i in range(3):
            for a in (0, 1):
                rows.append(
                    cat(
                        [
                            psi[i][32 * x + 16 * a : 32 * x + 16 * a + 16, 128 * par : 128 * par + 128]
                            for x in range(4)
                        ],
                        1,
                    )
                )
    return cat(rows, 0)


def stage_z_backward(t, grad):
    out = []
    for i in range(3):
        block = []
        for x in range(4):
            for a in (0, 1):
                block.append(
                    cat(
                        [
                            grad[
                                16 * (6 * par + 2 * i + a) : 16 * (6 * par + 2 * i + a) + 16,
                                128 * x : 128 * x + 128,
                            ]
                            for par in (0, 1)
                        ],
                        1,
                    )
                )
        field = cat(block, 0)
        o = table_left(nt, t["zb"], split(field), (1 if i == 2 else 0,))
        out.append(o.reshape(16, 16, 128))
    return jnp.stack(out, axis=1)


def stage_y_backward(t, got):
    tiles = [
        cat([got[8 * h + i, f] for f in range(3) for h in (0, 1)], 0).astype(F32) for i in range(8)
    ]
    tiles = transpose_groups(tiles)
    x = cat(
        [
            cat([tiles[i][16 * (2 * f + h) : 16 * (2 * f + h) + 16] for i in range(8)], 0)
            for f in range(3)
            for h in (0, 1)
        ],
        1,
    )
    pairs = [
        pair_swapped(nn(t["pb"][...], part).astype(BF), 128, 3) for part in parts_of(x, got.dtype)
    ]
    gx = table_right(nn, [p[0] for p in pairs], t["yt"])
    rest = table_right(nn, [cat(p[1:], 1) for p in pairs], t["yb"])
    parts = []
    for a in (0, 1):
        u, v = gx[:, 128 * a : 128 * a + 128], rest[:, 128 * a : 128 * a + 128]
        parts += [low_halves(u, v), high_halves(u, v)]
    return jnp.stack([p.reshape(8, 16, 128) for p in parts], axis=1).reshape(32, 16, 128)


def stage_x_backward(t, got, inverse, along):
    y = times_rows(table_left(nn, t["xb"], parts_of(got.reshape(512, 128), got.dtype)), along)
    modes = times_rows(y + roll(y, 64), inverse)
    o = table_left(nn, t["xj"], split(modes))
    return jnp.where(lanes() < 64, o[:256], o[256:]).reshape(32, 8, 128)


def stage_y_final(t, got):
    kind = got.dtype
    got = got.reshape(8, 4, 8, 128)
    tile = [got[:, i].reshape(64, 128) for i in range(4)]
    x = cat([f(tile[2 * a], tile[2 * a + 1]) for f in (low_halves, high_halves) for a in (0, 1)], 1)
    lefts = [
        cat(pair_swapped(nn(t["pj"][...], part).astype(BF), 64, 2), 0)
        for part in parts_of(x, kind)
    ]
    out = table_right(nn, lefts, t["yt"])
    first, second = out[:64], out[64:]
    parts = []
    for a in (0, 1):
        u, v = first[:, 128 * a : 128 * a + 128], second[:, 128 * a : 128 * a + 128]
        parts += [low_halves(u, v), high_halves(u, v)]
    return cat([p.reshape(4, 16, 128) for p in parts], 0)


def stage_z_final(t, got):
    return table_right(tn, parts_of(got.reshape(256, 128), got.dtype), t["zj"])


def iota2(shape, dim):
    return lax.broadcasted_iota(jnp.int32, shape, dim)


def down_weights(t, wd):
    eight = nt(t["e1"][...], wd).astype(BF)
    row, col = iota2((384, 192), 0), iota2((384, 192), 1)
    w = jnp.where(row // 48 == (col % 16) // 2, nt(eight, t["e2t"][...]), 0.0).astype(BF)
    row, col = iota2((192, 384), 0), iota2((192, 384), 1)
    wt = jnp.where(col // 48 == (row % 16) // 2, nt(t["e2t"][...], eight), 0.0).astype(BF)
    return w, wt


def out_weights(t, wo):
    wide = wo.astype(F32)
    each = cat([jnp.broadcast_to(wide[j : j + 1], (8, 48)) for j in range(3)], 0).astype(BF)
    row, col = iota2((24, 384), 0), iota2((24, 384), 1)
    w = jnp.where(row % 8 == col // 48, nt(each, t["e1"][...]), 0.0).astype(BF)
    row, col = iota2((384, 24), 0), iota2((384, 24), 1)
    wt = jnp.where(row // 48 == col % 8, nt(t["e1"][...], each), 0.0).astype(BF)
    return w, wt


def bias_rows(t, b):
    out, left = 0.0, b
    for _ in range(3):
        part = left.astype(BF)
        out = out + nt(t["e1"][...], jnp.broadcast_to(part.astype(F32), (128, 48)).astype(BF))
        left = left - part.astype(F32)
    return out


def place(i):
    return (iota2((48, 432), 1) == 48 * i + iota2((48, 432), 0)).astype(F32).astype(BF)


def conv_weights(wc):
    out = 0.0
    for i in range(9):
        out = out + nn(cat([wc[9 * dx + i] for dx in range(3)], 0), place(i))
    return out.astype(BF)


def conv_weights_back(wc):
    rows = []
    for ex in range(3):
        out = 0.0
        for i in range(9):
            out = out + tn(wc[26 - 9 * ex - i], place(i))
        rows.append(out)
    return cat(rows, 0).astype(BF)


def add_taps(o):
    return o[:48, :512] + o[48:96, 128:640] + o[96:, 256:]


def add_own_taps(o):
    none = jnp.zeros((48, 128), F32)
    return o[48:96] + cat([none, o[:48, :384]], 1) + cat([o[96:, 128:], none], 1)


def gate(v):
    return 0.5 + 0.5 * jnp.tanh(0.5 * v)


TABLES = tables()
NAMES = tuple(TABLES)


Q_AHEAD = sorted(
    [(dz, dc) for dz in range(8) for dc in range(2) if dz or dc],
    key=lambda t: -(min(t[0], 8 - t[0]) + 0.3 * t[1]),
)
R_AHEAD = sorted(
    [(dx, dy) for dx in range(4) for dy in range(8) if dx or dy],
    key=lambda t: -(min(t[0], 4 - t[0]) + min(t[1], 8 - t[1])),
)
rem = lax.rem
div = lax.div


def kernel(*refs):
    args = refs[:8]
    count = len(NAMES)
    source = dict(zip(NAMES, refs[8 : 8 + count]))
    out = refs[8 + count]
    rest = refs[9 + count :]
    t = dict(zip(NAMES, rest[:count]))
    rest = rest[count:]
    here, rest = rest[:8], rest[8:]
    den, wd, bd, wc, bc, wo, obs, noi = here
    (s1, r1, s2, r2, s3, r3, s4, r4, s5, r5, s6, r6, s7, r7, s8, r8) = rest[:16]
    (fb, gb, sb, w1, w2, wb, wbt, wp, wpt, slope, pc, got_obs, got_noi, fac, bias) = rest[16:31]
    tsem, asem, ssem, rsem, hsem_s, hsem_r, osem_s, osem_r = rest[31:]

    s = lax.axis_index("slab")
    zh = lax.axis_index("pencil")
    core = rem(s, 2)
    r = rem(div(s, 2), 32)
    zl = div(s, 64)
    z = 2 * zh + zl
    q = 2 * z + core
    rx, ry = div(r, 8), rem(r, 8)

    def device(q, r):
        return {"slab": 64 * rem(div(q, 2), 2) + 2 * r + rem(q, 2), "pencil": div(q, 4)}

    def q_partners():
        for dz, dc in Q_AHEAD:
            z2 = rem(z + dz, 8) if dz else z
            c2 = 1 - core if dc else core
            yield (
                2 * z2 + c2,
                {"slab": 64 * rem(z2, 2) + 2 * r + c2, "pencil": div(z2, 2)},
            )

    def r_partners():
        for dx, dy in R_AHEAD:
            x2 = rem(rx + dx, 4) if dx else rx
            y2 = rem(ry + dy, 8) if dy else ry
            r2 = 8 * x2 + y2
            yield r2, {"slab": 64 * zl + 2 * r2 + core, "pencil": zh}

    for i in (0, *range(1, 8)):
        pltpu.make_async_copy(args[i], here[i], asem.at[i]).start()
    for i, name in enumerate(NAMES):
        pltpu.make_async_copy(source[name], t[name], tsem.at[i]).start()

    barrier = pltpu.get_barrier_semaphore()

    def greet(dev):
        pl.semaphore_signal(barrier, inc=1, device_id=dev, device_id_type=MESH)

    for _, dev in r_partners():
        greet(dev)
    for _, dev in q_partners():
        greet(dev)
    for dq in (1, 15):
        for dr in (1, 31):
            greet(device(rem(q + dq, 16), rem(r + dr, 32)))
    home = div(s, 4)
    slot = rem(s, 4)
    mine = home == r
    own = mine.astype(jnp.int32)
    for j in range(4):

        @pl.when(jnp.logical_not(mine & (rem(q, 4) == j)))
        def _():
            greet(device(4 * zh + j, home))

        @pl.when(jnp.logical_not(mine & (slot == j)))
        def _():
            greet({"slab": 4 * r + j, "pencil": zh})

    def ready(*names):
        for name in names:
            pltpu.make_async_copy(source[name], t[name], tsem.at[NAMES.index(name)]).wait()

    def have(*numbers):
        for i in numbers:
            pltpu.make_async_copy(args[i], here[i], asem.at[i]).wait()

    def send(phase, src, dst, me, partners):
        for d, dev in partners:
            pltpu.make_async_remote_copy(
                src_ref=src.at[d],
                dst_ref=dst.at[me],
                send_sem=ssem.at[phase],
                recv_sem=rsem.at[phase],
                device_id=dev,
                device_id_type=MESH,
            ).start()
        dst[me] = src[me]

    def send_q(phase, src, dst):
        send(phase, src, dst, q, q_partners())

    def send_r(phase, src, dst):
        send(phase, src, dst, r, r_partners())

    def arrived(phase, dst):
        part = dst.at[pl.ds(0, dst.shape[0] - 1)]
        pltpu.make_async_copy(part, part, rsem.at[phase]).wait()

    def sent(phase, src):
        part = src.at[pl.ds(0, src.shape[0] - 1)]
        pltpu.make_async_copy(part, part, ssem.at[phase]).wait()

    def halo(which, buf, action):
        cut = {0: ((128, 640), (128, 640)), 1: ((512, 640), (0, 128)), -1: ((128, 256), (640, 768))}
        line = {0: ((1, 9), (1, 9)), 1: ((8, 9), (0, 1)), -1: ((1, 2), (9, 10))}
        ways = ((1, 0), (-1, 0), (1, 1), (1, -1), (-1, 1), (-1, -1), (0, 1), (0, -1))
        for k, (dr, dq) in enumerate(ways):
            (a, b), (c, d) = cut[dr]
            (e, f), (g, h) = line[dq]
            copy = pltpu.make_async_remote_copy(
                src_ref=buf.at[pl.ds(e, f - e), :, pl.ds(a, b - a)],
                dst_ref=buf.at[pl.ds(g, h - g), :, pl.ds(c, d - c)],
                send_sem=hsem_s.at[which, k],
                recv_sem=hsem_r.at[which, k],
                device_id=device(rem(q + dq + 16, 16), rem(r + dr + 32, 32)),
                device_id_type=MESH,
            )
            action(copy)

    def shifted(buf, rows, tiles):
        lo, hi = rows
        for x in tiles:
            part = buf[lo:hi, :, 128 * x : 128 * x + 128].reshape(48 * (hi - lo), 128)
            for dz, value in enumerate((roll(part, 1), part, roll(part, 127))):
                sb[lo:hi, 48 * dz : 48 * dz + 48, 128 * x : 128 * x + 128] = value.reshape(
                    hi - lo, 48, 128
                )

    def conv(which, buf, weights):
        shifted(buf, (1, 9), range(1, 5))

        def inner(y, carry):
            o = nn(weights[...], sb[pl.ds(y, 3), :, 128:640].reshape(432, 512))
            pc[y] = add_own_taps(o)
            return carry

        lax.fori_loop(1, 7, inner, 0)
        halo(which, buf, lambda c: c.wait_recv())
        shifted(buf, (0, 10), (0, 5))
        shifted(buf, (0, 1), range(1, 5))
        shifted(buf, (9, 10), range(1, 5))

        def edges(y, carry):
            side = cat([sb[pl.ds(y, 3), :, 0:128], sb[pl.ds(y, 3), :, 640:768]], 2)
            o = nn(weights[...], side.reshape(432, 256))
            pc[y, :, 0:128] += o[:48, :128]
            pc[y, :, 384:512] += o[96:, 128:]
            return carry

        lax.fori_loop(1, 7, edges, 0)
        for y in (0, 7):
            pc[y] = add_taps(nn(weights[...], sb[y : y + 3].reshape(432, 768)))

    have(0)
    ready("zf")
    s1[...] = (stage_z_forward(t, den[...].reshape(128, 256))).astype(s1.dtype)
    have(6, 7)
    pl.semaphore_wait(barrier, 58 - 2 * own)
    send_q(0, s1, r1)

    def observed_copies(j, action):
        for src, dst, kind in (
            (obs.at[:, 0, pl.ds(8 * j, 8), :], got_obs.at[slot], 0),
            (noi.at[0, pl.ds(8 * j, 8), :], got_noi.at[slot], 1),
        ):
            action(
                pltpu.make_async_remote_copy(
                    src_ref=src,
                    dst_ref=dst,
                    send_sem=osem_s.at[kind, j],
                    recv_sem=osem_r.at[kind, slot],
                    device_id=device(4 * zh + j, home),
                    device_id_type=MESH,
                )
            )

    for j in range(4):
        this = mine & (rem(q, 4) == j)

        @pl.when(jnp.logical_not(this))
        def _():
            observed_copies(j, lambda c: c.start())

        @pl.when(this)
        def _():
            got_obs[slot] = obs[:, 0, 8 * j : 8 * j + 8, :]
            got_noi[slot] = noi[0, 8 * j : 8 * j + 8, :]

    inverse, both, along = factors(q, r)
    fac[0] = inverse
    fac[1] = both
    fac[2] = along
    ready("e1", "e2t")
    have(1, 2, 3, 4, 5)
    w, wt = down_weights(t, wd[...])
    wb[...] = w
    wbt[...] = wt
    w, wt = out_weights(t, wo[...])
    wp[...] = w
    wpt[...] = wt
    bias[0] = bias_rows(t, bd[...])
    bias[1] = bias_rows(t, bc[...])

    arrived(0, r1)
    ready("pf", "yt")
    s2[...] = (stage_y_forward(t, r1[...])).astype(s2.dtype)
    send_r(1, s2, r2)
    w1[...] = conv_weights(wc)
    arrived(1, r2)
    ready("xf", "xi")
    s3[...] = (stage_x_forward(t, r2[...], fac[1])).astype(s3.dtype)
    send_r(2, s3, r3)
    w2[...] = conv_weights_back(wc)
    arrived(2, r3)
    ready("pi", "yi")
    s4[...] = (stage_y_inverse(t, r3[...])).astype(s4.dtype)
    send_q(3, s4, r4)
    ready("zi", "zb", "pb", "yb", "xb", "xj", "pj", "zj")
    arrived(3, r4)

    cells = stage_z_inverse(t, r4[...])
    v = nn(wb[...], cells) + cat([bias[0]] * 4, 1)
    g = gate(v)
    fb[1:9, :, 128:640] = (v * g).astype(BF).reshape(8, 48, 512)
    halo(0, fb, lambda c: c.start())
    slope[...] = g * (1.0 + v * (1.0 - g))
    conv(0, fb, w1)

    for j in range(4):

        @pl.when(jnp.logical_not(mine & (slot == j)))
        def _():
            pltpu.make_async_copy(got_obs.at[j], got_obs.at[j], osem_r.at[0, j]).wait()
            pltpu.make_async_copy(got_noi.at[j], got_noi.at[j], osem_r.at[1, j]).wait()

    v = pc[...].reshape(384, 512) + cat([bias[1]] * 4, 1)
    g = gate(v)
    hidden = (v * g).astype(BF)
    predicted = nn(wp[...], hidden)
    seen = cat([got_obs[x].reshape(24, 128) for x in range(4)], 1)
    weight = cat([cat([got_noi[x]] * 3, 0) for x in range(4)], 1)
    residual = weight * (predicted - seen)
    high, low = split(residual)
    back = nn(wpt[...], high) + nn(wpt[...], low)
    grad_conv = (back * (g * (1.0 + v * (1.0 - g)))).astype(BF)
    gb[1:9, :, 128:640] = grad_conv.reshape(8, 48, 512)
    halo(1, gb, lambda c: c.start())
    conv(1, gb, w2)
    grad_down = (pc[...].reshape(384, 512) * slope[...]).astype(BF)
    s5[...] = (stage_z_backward(t, nn(wbt[...], grad_down))).astype(s5.dtype)

    send_q(4, s5, r5)
    arrived(4, r5)
    s6[...] = (stage_y_backward(t, r5[...])).astype(s6.dtype)
    send_r(5, s6, r6)
    arrived(5, r6)
    s7[...] = (stage_x_backward(t, r6[...], fac[0], fac[2])).astype(s7.dtype)
    send_r(6, s7, r7)
    arrived(6, r7)
    s8[...] = (stage_y_final(t, r7[...])).astype(s8.dtype)
    send_q(7, s8, r8)
    for phase, ref in enumerate((s1, s2, s3, s4, s5, s6, s7)):
        sent(phase, ref)
    halo(0, fb, lambda c: c.wait_send())
    halo(1, gb, lambda c: c.wait_send())
    for j in range(4):

        @pl.when(jnp.logical_not(mine & (rem(q, 4) == j)))
        def _():
            observed_copies(j, lambda c: c.wait_send())

    arrived(7, r8)
    out[...] = stage_z_final(t, r8[...]).reshape(2, 64, 256)
    sent(7, s8)


def on_device(
    density, weight_down, bias_down, weight_conv, bias_conv, weight_out, observed, noise_precision
):
    vmem = pl.BlockSpec(memory_space=pltpu.VMEM)
    shapes = [(v.shape, BF) for v in TABLES.values()]
    inputs = (
        density,
        weight_down.T,
        bias_down.reshape(1, -1),
        weight_conv,
        bias_conv.reshape(1, -1),
        weight_out,
        observed,
        noise_precision,
    )
    shapes += [(v.shape, v.dtype) for v in inputs]
    wide, one = (16, 16, 128), (32, 8, 128)
    two, three = (32, 16, 128), (16, 3, 16, 128)
    for shape, kind in zip((wide, one, two, three, three, two, one, wide), KINDS):
        shapes += [(shape, kind)] * 2
    shapes += [
        ((10, 48, 768), BF),
        ((10, 48, 768), BF),
        ((10, 144, 768), BF),
        ((144, 432), BF),
        ((144, 432), BF),
        ((384, 192), BF),
        ((192, 384), BF),
        ((24, 384), BF),
        ((384, 24), BF),
        ((384, 512), F32),
        ((8, 48, 512), F32),
        ((4, 3, 8, 128), F32),
        ((4, 8, 128), F32),
        ((3, N, 128), F32),
        ((2, 384, 128), F32),
    ]
    dma = pltpu.SemaphoreType.DMA
    return pl.pallas_call(
        kernel,
        out_shape=jax.ShapeDtypeStruct((2, 64, 256), F32),
        in_specs=[pl.BlockSpec(memory_space=pltpu.HBM)] * (8 + len(NAMES)),
        out_specs=vmem,
        scratch_shapes=[pltpu.VMEM(shape, kind) for shape, kind in shapes]
        + [
            dma((len(NAMES),)),
            dma((8,)),
            dma((8,)),
            dma((8,)),
            dma((2, 8)),
            dma((2, 8)),
            dma((2, 4)),
            dma((2, 4)),
        ],
        compiler_params=pltpu.CompilerParams(
            collective_id=0, has_side_effects=True, vmem_limit_bytes=64 * 1024 * 1024
        ),
    )(
        *inputs,
        *[jnp.asarray(TABLES[name]) for name in NAMES],
    )


def solution(mesh):
    return jax.shard_map(
        on_device,
        mesh=mesh,
        in_specs=(
            P("slab", "pencil", None),
            P(),
            P(),
            P(),
            P(),
            P(),
            P(None, "slab", "pencil", None),
            P("slab", "pencil", None),
        ),
        out_specs=P("slab", "pencil", None),
        check_vma=False,
    )
```

```python
import functools

import jax
import jax.numpy as jnp
import ml_dtypes
import numpy as np
from jax import lax
from jax.experimental import pallas as pl
from jax.experimental.pallas import tpu as pltpu
from jax.sharding import PartitionSpec as P

MESH = pl.DeviceIdType.MESH
BF = jnp.bfloat16
F32 = jnp.float32
N = 256
GROWTH = 3.0
TWO_PI = 2.0 * np.pi
KINDS = (F32, F32, F32, F32, BF, F32, F32, F32)


def theta(a, b):
    return TWO_PI * ((a[:, None].astype(np.int64) * b[None, :]) % N) / N


def grid(*sizes):
    return [g.reshape(-1) for g in np.meshgrid(*[np.arange(s) for s in sizes], indexing="ij")]


def signed(k):
    return np.where(k < N // 2, k, k - N)


def wave(k):
    return np.where(k == N // 2, 0, signed(k)) * (TWO_PI / N)


def complex_rows(angle, c_out, c_in, sign, turn):
    value = np.exp(1j * sign * angle) * (1j**turn)
    a, b = c_out[:, None], c_in[None, :]
    same = a == b
    cross = np.where((a == 0) & (b == 1), -value.imag, value.imag)
    return np.where(same, value.real, cross)


def swap_rows(order_in, order_out, sign):
    rows_in = {key: i for i, key in enumerate(order_in)}
    count = len(order_in)
    out = np.zeros((2 * count, count))
    for i, key in enumerate(order_out):
        out[i, rows_in[key]] = 1.0
        name = dict(key)
        name["c"] = 1 - name["c"]
        other = tuple(name.items())
        out[count + i, rows_in[other]] = (1.0 if dict(key)["c"] == 0 else -1.0) * (-sign)
    return out


def keys(spec, canon):
    names = [n for n, _ in spec]
    axes = grid(*[s for _, s in spec])
    out = []
    for values in zip(*axes):
        d = dict(zip(names, (int(v) for v in values)))
        out.append(tuple((n, d[n]) for n in canon))
    return out


def tables():
    t = {}
    half = np.where(np.arange(N // 2) == 0, 1.0, 2.0) / float(N) ** 3
    z = np.arange(N)
    q, c, k = grid(16, 2, 8)
    kz = 8 * q + k
    t["zf"] = complex_rows(theta(kz, z), c, np.zeros(N, np.int64), -1, 0)
    par, zz = grid(2, 128)
    zc = 2 * zz + par
    back = complex_rows(theta(kz, zc), c, np.zeros(N, np.int64), -1, 0) * half[kz][:, None]
    t["zb"] = np.stack([back, back * wave(kz)[:, None]])
    q, k, c = grid(16, 8, 2)
    kz = 8 * q + k
    inv = complex_rows(theta(kz, zc).T, np.zeros(N, np.int64), c, 1, 0).T * half[kz][:, None]
    t["zi"] = np.stack([inv, inv * wave(kz)[:, None]])
    t["zj"] = complex_rows(theta(kz, z).T, np.zeros(N, np.int64), c, 1, 0).T
    a = np.arange(N)
    base = np.concatenate([np.cos(theta(a, a)), np.sin(theta(a, a))], axis=0)
    qy = wave(a)
    t["yt"] = base
    times = np.concatenate([qy, qy])[:, None] * base
    t["yi"] = np.concatenate([times, base], axis=1)
    by = base * qy[None, :]
    t["yb"] = np.concatenate([by, base], axis=0)
    par, c_k, k2 = grid(2, 2, N // 2)
    kx = 2 * k2 + par
    r, w, c_in = grid(32, 4, 2)
    pos = lambda x1: 128 * (w // 2) + 4 * r + 2 * (w % 2) + x1
    t["xf"] = np.concatenate(
        [complex_rows(theta(kx, pos(v)), c_k, c_in, -1, 0) for v in (0, 1)], axis=0
    )
    t["xj"] = np.concatenate(
        [complex_rows(theta(kx, pos(v)).T, c_in, c_k, 1, -1) for v in (0, 1)], axis=0
    )
    c_h, k2 = grid(2, N // 2)
    r, c, x8 = grid(16, 2, 8)
    t["xi"] = np.stack(
        [complex_rows(theta(2 * k2 + p, 8 * r + x8).T, c, c_h, 1, 1) for p in (0, 1)]
    )
    r, x8, c = grid(16, 8, 2)
    t["xb"] = np.stack(
        [complex_rows(theta(2 * k2 + p, 8 * r + x8), c_h, c, -1, 0) for p in (0, 1)]
    )
    pairs = {}
    for name, value in t.items():
        high = value.astype(np.float32).astype(ml_dtypes.bfloat16)
        low = (value - high.astype(np.float64)).astype(np.float32).astype(ml_dtypes.bfloat16)
        pairs[name] = np.stack([high, low])
    canon = ("w", "c", "k")
    s = {}
    s["pf"] = swap_rows(
        keys((("w", 4), ("c", 2), ("k", 8)), canon), keys((("k", 8), ("w", 4), ("c", 2)), canon), -1
    )
    s["pj"] = swap_rows(
        keys((("k", 8), ("w", 4), ("c", 2)), canon), keys((("w", 4), ("k", 8), ("c", 2)), canon), 1
    )
    s["pi"] = swap_rows(
        keys((("k", 8), ("c", 2), ("w", 8)), canon), keys((("w", 8), ("k", 8), ("c", 2)), canon), 1
    )
    s["pb"] = swap_rows(
        keys((("w", 8), ("c", 2), ("k", 8)), canon), keys((("k", 8), ("w", 8), ("c", 2)), canon), -1
    )
    par, i, a, y = grid(2, 3, 2, 16)
    e2 = np.zeros((192, 24))
    e2[np.arange(192), 8 * i + 4 * a + 2 * (y % 2) + par] = 1.0
    s["e2t"] = e2
    e1 = np.zeros((384, 48))
    e1[np.arange(384), np.arange(384) % 48] = 1.0
    s["e1"] = e1
    for name, value in s.items():
        pairs[name] = value.astype(np.float32).astype(ml_dtypes.bfloat16)
    return pairs


def dot(a, b, ca, cb):
    return lax.dot_general(a, b, (((ca,), (cb,)), ((), ())), preferred_element_type=F32)


def nn(a, b):
    return dot(a, b, 1, 0)


def nt(a, b):
    return dot(a, b, 1, 1)


def tn(a, b):
    return dot(a, b, 0, 0)


def roll(x, shift):
    return pltpu.roll(x, shift % x.shape[-1], x.ndim - 1)


def split(x):
    high = x.astype(BF)
    return high, (x - high.astype(F32)).astype(BF)


def lanes():
    return lax.broadcasted_iota(jnp.int32, (1, 128), 1)


def low_halves(a, b):
    return jnp.where(lanes() < 64, a, roll(b, 64))


def high_halves(a, b):
    return jnp.where(lanes() < 64, roll(a, 64), b)


def transpose_groups(tiles):
    tiles = list(tiles)
    for d in (1, 2, 4):
        odd = (lanes() // (16 * d)) % 2 == 1
        for i in range(8):
            if i & d:
                continue
            low, high = tiles[i], tiles[i + d]
            tiles[i] = jnp.where(odd, roll(high, 16 * d), low)
            tiles[i + d] = jnp.where(odd, high, roll(low, 128 - 16 * d))
    return tiles


def cat(parts, axis):
    return jnp.concatenate(list(parts), axis=axis)


def parts_of(x, kind):
    return (x.astype(BF),) if kind == BF else split(x)


def pair_swapped(moved, rows, fields):
    return [
        cat([moved[:rows, 256 * f : 256 * f + 256], moved[rows:, 256 * f : 256 * f + 256]], 1)
        for f in range(fields)
    ]


def table_left(form, t, x, index=()):
    high, low = t[(0, *index)], t[(1, *index)]
    out = form(high, x[0]) + form(low, x[0])
    if len(x) > 1:
        out = out + form(high, x[1])
    return out


def table_right(form, x, t, index=()):
    high, low = t[(0, *index)], t[(1, *index)]
    out = form(x[0], high) + form(x[0], low)
    if len(x) > 1:
        out = out + form(x[1], high)
    return out


def stage_z_forward(t, density):
    return table_left(nt, t["zf"], split(density)).reshape(16, 16, 128)


def stage_y_forward(t, got):
    z_rows = [got[4 * i : 4 * i + 4].reshape(64, 128).astype(F32) for i in range(4)]
    x = cat(
        [f(z_rows[2 * a], z_rows[2 * a + 1]) for f in (low_halves, high_halves) for a in (0, 1)], 1
    )
    left = [
        cat(pair_swapped(nn(t["pf"][...], part).astype(BF), 64, 2), 0)
        for part in parts_of(x, got.dtype)
    ]
    out = table_right(nn, left, t["yt"])
    first, second = out[:64], out[64:]
    parts = []
    for a in (0, 1):
        u, v = first[:, 128 * a : 128 * a + 128], second[:, 128 * a : 128 * a + 128]
        parts += [low_halves(u, v), high_halves(u, v)]
    return jnp.stack([p.reshape(8, 8, 128) for p in parts], axis=1).reshape(32, 8, 128)


def factors(q, r):
    kz = 8 * q + r // 4
    row = lax.broadcasted_iota(jnp.int32, (N, 128), 0)
    lane = lax.broadcasted_iota(jnp.int32, (N, 128), 1)
    ky = 64 * (r % 4) + lane % 64
    spacing = F32(TWO_PI / N)

    kx = 2 * (row % 128) + row // 128

    def full(k):
        return jnp.where(k < N // 2, k, k - N).astype(F32) * spacing

    fx, fy = full(kx), full(ky)
    fz = (kz + 0 * row).astype(F32) * spacing
    square = fx * fx + fy * fy + fz * fz
    anchor = (kx == 0) & (ky == 0) & (kz == 0)
    square = jnp.where(anchor, F32(1.0), square)
    qx = jnp.where(kx == N // 2, F32(0.0), fx)
    first = lane < 64
    inverse = F32(GROWTH) / square
    return inverse, jnp.where(first, inverse, inverse * qx), jnp.where(first, qx, F32(1.0))


def times_rows(x, factor):
    half = N // 2
    return (x.reshape(2, 2, half, 128) * factor.reshape(2, 1, half, 128)).reshape(2 * N, 128)


def stage_x_forward(t, got, factor):
    y = table_left(nn, t["xf"], split(got.reshape(256, 128)))
    z = jnp.where(lanes() < 64, y[:512], y[512:])
    modes = times_rows(z + roll(z, 64), factor)
    even = table_left(nn, t["xi"], split(modes[:256]), (0,))
    odd = table_left(nn, t["xi"], split(modes[256:]), (1,))
    return cat([even + odd, even - odd], 0).reshape(32, 16, 128)


def stage_y_inverse(t, got):
    kind = got.dtype
    got = got.reshape(8, 4, 16, 128)
    tile = [got[:, i].reshape(128, 128).astype(F32) for i in range(4)]
    x = cat([f(tile[2 * a], tile[2 * a + 1]) for f in (low_halves, high_halves) for a in (0, 1)], 1)
    left = [
        pair_swapped(nn(t["pi"][...], part).astype(BF), 128, 2) for part in parts_of(x, kind)
    ]
    ox = table_right(nn, [p[1] for p in left], t["yt"])
    oyz = table_right(nn, [p[0] for p in left], t["yi"])
    fields = (ox, oyz[:, :256], oyz[:, 256:])
    tiles = [
        cat([f[16 * i : 16 * i + 16, 128 * h : 128 * h + 128] for f in fields for h in (0, 1)], 0)
        for i in range(8)
    ]
    tiles = transpose_groups(tiles)
    return jnp.stack(
        [tiles[i].reshape(3, 2, 16, 128)[:, h] for h in (0, 1) for i in range(8)], axis=0
    )


def stage_z_inverse(t, got):
    psi = []
    for i in range(3):
        m = got[:, i].reshape(256, 128)
        psi.append(
            table_right(tn, parts_of(m, got.dtype), t["zi"], (1 if i == 2 else 0,)).astype(BF)
        )
    rows = []
    for par in (0, 1):
        for i in range(3):
            for a in (0, 1):
                rows.append(
                    cat(
                        [
                            psi[i][32 * x + 16 * a : 32 * x + 16 * a + 16, 128 * par : 128 * par + 128]
                            for x in range(4)
                        ],
                        1,
                    )
                )
    return cat(rows, 0)


def stage_z_backward(t, grad):
    out = []
    for i in range(3):
        block = []
        for x in range(4):
            for a in (0, 1):
                block.append(
                    cat(
                        [
                            grad[
                                16 * (6 * par + 2 * i + a) : 16 * (6 * par + 2 * i + a) + 16,
                                128 * x : 128 * x + 128,
                            ]
                            for par in (0, 1)
                        ],
                        1,
                    )
                )
        field = cat(block, 0)
        o = table_left(nt, t["zb"], split(field), (1 if i == 2 else 0,))
        out.append(o.reshape(16, 16, 128))
    return jnp.stack(out, axis=1)


def stage_y_backward(t, got):
    tiles = [
        cat([got[8 * h + i, f] for f in range(3) for h in (0, 1)], 0).astype(F32) for i in range(8)
    ]
    tiles = transpose_groups(tiles)
    x = cat(
        [
            cat([tiles[i][16 * (2 * f + h) : 16 * (2 * f + h) + 16] for i in range(8)], 0)
            for f in range(3)
            for h in (0, 1)
        ],
        1,
    )
    pairs = [
        pair_swapped(nn(t["pb"][...], part).astype(BF), 128, 3) for part in parts_of(x, got.dtype)
    ]
    gx = table_right(nn, [p[0] for p in pairs], t["yt"])
    rest = table_right(nn, [cat(p[1:], 1) for p in pairs], t["yb"])
    parts = []
    for a in (0, 1):
        u, v = gx[:, 128 * a : 128 * a + 128], rest[:, 128 * a : 128 * a + 128]
        parts += [low_halves(u, v), high_halves(u, v)]
    return jnp.stack([p.reshape(8, 16, 128) for p in parts], axis=1).reshape(32, 16, 128)


def stage_x_backward(t, got, inverse, along):
    planes = got.reshape(512, 128).astype(F32)
    low, high = planes[:256], planes[256:]
    even = table_left(nn, t["xb"], split(low + high), (0,))
    odd = table_left(nn, t["xb"], split(low - high), (1,))
    y = times_rows(cat([even, odd], 0), along)
    modes = times_rows(y + roll(y, 64), inverse)
    o = table_left(nn, t["xj"], split(modes))
    return jnp.where(lanes() < 64, o[:256], o[256:]).reshape(32, 8, 128)


def stage_y_final(t, got):
    kind = got.dtype
    got = got.reshape(8, 4, 8, 128)
    tile = [got[:, i].reshape(64, 128) for i in range(4)]
    x = cat([f(tile[2 * a], tile[2 * a + 1]) for f in (low_halves, high_halves) for a in (0, 1)], 1)
    lefts = [
        cat(pair_swapped(nn(t["pj"][...], part).astype(BF), 64, 2), 0)
        for part in parts_of(x, kind)
    ]
    out = table_right(nn, lefts, t["yt"])
    first, second = out[:64], out[64:]
    parts = []
    for a in (0, 1):
        u, v = first[:, 128 * a : 128 * a + 128], second[:, 128 * a : 128 * a + 128]
        parts += [low_halves(u, v), high_halves(u, v)]
    return cat([p.reshape(4, 16, 128) for p in parts], 0)


def stage_z_final(t, got):
    return table_right(tn, parts_of(got.reshape(256, 128), got.dtype), t["zj"])


def iota2(shape, dim):
    return lax.broadcasted_iota(jnp.int32, shape, dim)


def down_weights(t, wd):
    eight = nt(t["e1"][...], wd).astype(BF)
    row, col = iota2((384, 192), 0), iota2((384, 192), 1)
    w = jnp.where(row // 48 == (col % 16) // 2, nt(eight, t["e2t"][...]), 0.0).astype(BF)
    row, col = iota2((192, 384), 0), iota2((192, 384), 1)
    wt = jnp.where(col // 48 == (row % 16) // 2, nt(t["e2t"][...], eight), 0.0).astype(BF)
    return w, wt


def out_weights(t, wo):
    wide = wo.astype(F32)
    each = cat([jnp.broadcast_to(wide[j : j + 1], (8, 48)) for j in range(3)], 0).astype(BF)
    row, col = iota2((24, 384), 0), iota2((24, 384), 1)
    w = jnp.where(row % 8 == col // 48, nt(each, t["e1"][...]), 0.0).astype(BF)
    row, col = iota2((384, 24), 0), iota2((384, 24), 1)
    wt = jnp.where(row // 48 == col % 8, nt(t["e1"][...], each), 0.0).astype(BF)
    return w, wt


def bias_rows(t, b):
    out, left = 0.0, b
    for _ in range(3):
        part = left.astype(BF)
        out = out + nt(t["e1"][...], jnp.broadcast_to(part.astype(F32), (128, 48)).astype(BF))
        left = left - part.astype(F32)
    return out


def place(i):
    return (iota2((48, 432), 1) == 48 * i + iota2((48, 432), 0)).astype(F32).astype(BF)


def conv_weights(wc):
    out = 0.0
    for i in range(9):
        out = out + nn(cat([wc[9 * dx + i] for dx in range(3)], 0), place(i))
    return out.astype(BF)


def conv_weights_back(wc):
    rows = []
    for ex in range(3):
        out = 0.0
        for i in range(9):
            out = out + tn(wc[26 - 9 * ex - i], place(i))
        rows.append(out)
    return cat(rows, 0).astype(BF)


def add_taps(o):
    return o[:48, :512] + o[48:96, 128:640] + o[96:, 256:]


def add_own_taps(o):
    none = jnp.zeros((48, 128), F32)
    return o[48:96] + cat([none, o[:48, :384]], 1) + cat([o[96:, 128:], none], 1)


def gate(v):
    return 0.5 + 0.5 * jnp.tanh(0.5 * v)


TABLES = tables()
NAMES = tuple(TABLES)


Q_AHEAD = sorted(
    [(dz, dc) for dz in range(8) for dc in range(2) if dz or dc],
    key=lambda t: -(min(t[0], 8 - t[0]) + 0.3 * t[1]),
)
R_AHEAD = sorted(
    [(dx, dy) for dx in range(4) for dy in range(8) if dx or dy],
    key=lambda t: -(min(t[0], 4 - t[0]) + min(t[1], 8 - t[1])),
)
rem = lax.rem
div = lax.div


def kernel(*refs):
    args = refs[:8]
    count = len(NAMES)
    source = dict(zip(NAMES, refs[8 : 8 + count]))
    out = refs[8 + count]
    rest = refs[9 + count :]
    t = dict(zip(NAMES, rest[:count]))
    rest = rest[count:]
    here, rest = rest[:8], rest[8:]
    den, wd, bd, wc, bc, wo, obs, noi = here
    (s1, r1, s2, r2, s3, r3, s4, r4, s5, r5, s6, r6, s7, r7, s8, r8) = rest[:16]
    (fb, gb, sb, w1, w2, wb, wbt, wp, wpt, slope, pc, got_obs, got_noi, fac, bias) = rest[16:31]
    tsem, asem, ssem, rsem, hsem_s, hsem_r, osem_s, osem_r = rest[31:]

    s = lax.axis_index("slab")
    zh = lax.axis_index("pencil")
    core = rem(s, 2)
    r = rem(div(s, 2), 32)
    zl = div(s, 64)
    z = 2 * zh + zl
    q = 2 * z + core
    rx, ry = div(r, 8), rem(r, 8)

    def device(q, r):
        return {"slab": 64 * rem(div(q, 2), 2) + 2 * r + rem(q, 2), "pencil": div(q, 4)}

    def q_partners():
        for dz, dc in Q_AHEAD:
            z2 = rem(z + dz, 8) if dz else z
            c2 = 1 - core if dc else core
            yield (
                2 * z2 + c2,
                {"slab": 64 * rem(z2, 2) + 2 * r + c2, "pencil": div(z2, 2)},
            )

    def r_partners():
        for dx, dy in R_AHEAD:
            x2 = rem(rx + dx, 4) if dx else rx
            y2 = rem(ry + dy, 8) if dy else ry
            r2 = 8 * x2 + y2
            yield r2, {"slab": 64 * zl + 2 * r2 + core, "pencil": zh}

    first = NAMES.index("zf")

    def load(i):
        pltpu.make_async_copy(args[i], here[i], asem.at[i]).start()

    def load_table(i):
        pltpu.make_async_copy(source[NAMES[i]], t[NAMES[i]], tsem.at[i]).start()

    load(0)
    load_table(first)

    barrier = pltpu.get_barrier_semaphore()

    def greet(dev):
        pl.semaphore_signal(barrier, inc=1, device_id=dev, device_id_type=MESH)

    for _, dev in r_partners():
        greet(dev)
    for _, dev in q_partners():
        greet(dev)
    for dq in (1, 15):
        for dr in (1, 31):
            greet(device(rem(q + dq, 16), rem(r + dr, 32)))
    home = div(s, 4)
    slot = rem(s, 4)
    mine = home == r
    own = mine.astype(jnp.int32)
    for j in range(4):

        @pl.when(jnp.logical_not(mine & (rem(q, 4) == j)))
        def _():
            greet(device(4 * zh + j, home))

        @pl.when(jnp.logical_not(mine & (slot == j)))
        def _():
            greet({"slab": 4 * r + j, "pencil": zh})

    for i in (6, 7, *range(1, 6)):
        load(i)
    for i in range(len(NAMES)):
        if i != first:
            load_table(i)

    def ready(*names):
        for name in names:
            pltpu.make_async_copy(source[name], t[name], tsem.at[NAMES.index(name)]).wait()

    def have(*numbers):
        for i in numbers:
            pltpu.make_async_copy(args[i], here[i], asem.at[i]).wait()

    def send(phase, src, dst, me, partners):
        for d, dev in partners:
            pltpu.make_async_remote_copy(
                src_ref=src.at[d],
                dst_ref=dst.at[me],
                send_sem=ssem.at[phase],
                recv_sem=rsem.at[phase],
                device_id=dev,
                device_id_type=MESH,
            ).start()
        dst[me] = src[me]

    def send_q(phase, src, dst):
        send(phase, src, dst, q, q_partners())

    def send_r(phase, src, dst):
        send(phase, src, dst, r, r_partners())

    def arrived(phase, dst):
        part = dst.at[pl.ds(0, dst.shape[0] - 1)]
        pltpu.make_async_copy(part, part, rsem.at[phase]).wait()

    def sent(phase, src):
        part = src.at[pl.ds(0, src.shape[0] - 1)]
        pltpu.make_async_copy(part, part, ssem.at[phase]).wait()

    def halo(which, buf, action):
        cut = {0: ((1, 5), (1, 5)), 1: ((4, 5), (0, 1)), -1: ((1, 2), (5, 6))}
        line = {0: ((1, 9), (1, 9)), 1: ((8, 9), (0, 1)), -1: ((1, 2), (9, 10))}
        ways = ((1, 0), (-1, 0), (1, 1), (1, -1), (-1, 1), (-1, -1), (0, 1), (0, -1))
        for k, (dr, dq) in enumerate(ways):
            (a, b), (c, d) = cut[dr]
            (e, f), (g, h) = line[dq]
            copy = pltpu.make_async_remote_copy(
                src_ref=buf.at[pl.ds(a, b - a), pl.ds(e, f - e)],
                dst_ref=buf.at[pl.ds(c, d - c), pl.ds(g, h - g)],
                send_sem=hsem_s.at[which, k],
                recv_sem=hsem_r.at[which, k],
                device_id=device(rem(q + dq + 16, 16), rem(r + dr + 32, 32)),
                device_id_type=MESH,
            )
            action(copy)

    def shifted(buf, rows, tiles):
        lo, hi = rows
        for x in tiles:
            part = buf[x, lo:hi].reshape(48 * (hi - lo), 128)
            for dz, value in enumerate((roll(part, 1), part, roll(part, 127))):
                sb[lo:hi, 48 * dz : 48 * dz + 48, 128 * x : 128 * x + 128] = value.reshape(
                    hi - lo, 48, 128
                )

    def fill(buf, value):
        for x in range(4):
            buf[x + 1, 1:9] = value[:, 128 * x : 128 * x + 128].reshape(8, 48, 128)

    def conv(which, buf, weights):
        shifted(buf, (1, 9), range(1, 5))

        def inner(y, carry):
            o = nn(weights[...], sb[pl.ds(y, 3), :, 128:640].reshape(432, 512))
            pc[y] = add_own_taps(o)
            return carry

        lax.fori_loop(1, 7, inner, 0)
        halo(which, buf, lambda c: c.wait_recv())
        shifted(buf, (0, 10), (0, 5))
        shifted(buf, (0, 1), range(1, 5))
        shifted(buf, (9, 10), range(1, 5))

        def edges(y, carry):
            side = cat([sb[pl.ds(y, 3), :, 0:128], sb[pl.ds(y, 3), :, 640:768]], 2)
            o = nn(weights[...], side.reshape(432, 256))
            pc[y, :, 0:128] += o[:48, :128]
            pc[y, :, 384:512] += o[96:, 128:]
            return carry

        lax.fori_loop(1, 7, edges, 0)
        for y in (0, 7):
            pc[y] = add_taps(nn(weights[...], sb[y : y + 3].reshape(432, 768)))

    have(0)
    ready("zf")
    s1[...] = (stage_z_forward(t, den[...].reshape(128, 256))).astype(s1.dtype)
    have(6, 7)
    pl.semaphore_wait(barrier, 58 - 2 * own)
    send_q(0, s1, r1)

    def observed_copies(j, action):
        for src, dst, kind in (
            (obs.at[:, 0, pl.ds(8 * j, 8), :], got_obs.at[slot], 0),
            (noi.at[0, pl.ds(8 * j, 8), :], got_noi.at[slot], 1),
        ):
            action(
                pltpu.make_async_remote_copy(
                    src_ref=src,
                    dst_ref=dst,
                    send_sem=osem_s.at[kind, j],
                    recv_sem=osem_r.at[kind, slot],
                    device_id=device(4 * zh + j, home),
                    device_id_type=MESH,
                )
            )

    for j in range(4):
        this = mine & (rem(q, 4) == j)

        @pl.when(jnp.logical_not(this))
        def _():
            observed_copies(j, lambda c: c.start())

        @pl.when(this)
        def _():
            got_obs[slot] = obs[:, 0, 8 * j : 8 * j + 8, :]
            got_noi[slot] = noi[0, 8 * j : 8 * j + 8, :]

    inverse, both, along = factors(q, r)
    fac[0] = inverse
    fac[1] = both
    fac[2] = along
    ready("e1", "e2t")
    have(1, 2, 3, 4, 5)
    w, wt = down_weights(t, wd[...])
    wb[...] = w
    wbt[...] = wt
    w, wt = out_weights(t, wo[...])
    wp[...] = w
    wpt[...] = wt
    bias[0] = bias_rows(t, bd[...])
    bias[1] = bias_rows(t, bc[...])

    arrived(0, r1)
    ready("pf", "yt")
    s2[...] = (stage_y_forward(t, r1[...])).astype(s2.dtype)
    send_r(1, s2, r2)
    w1[...] = conv_weights(wc)
    arrived(1, r2)
    ready("xf", "xi")
    s3[...] = (stage_x_forward(t, r2[...], fac[1])).astype(s3.dtype)
    send_r(2, s3, r3)
    w2[...] = conv_weights_back(wc)
    arrived(2, r3)
    ready("pi", "yi")
    s4[...] = (stage_y_inverse(t, r3[...])).astype(s4.dtype)
    send_q(3, s4, r4)
    ready("zi", "zb", "pb", "yb", "xb", "xj", "pj", "zj")
    arrived(3, r4)

    cells = stage_z_inverse(t, r4[...])
    v = nn(wb[...], cells) + cat([bias[0]] * 4, 1)
    g = gate(v)
    fill(fb, (v * g).astype(BF))
    halo(0, fb, lambda c: c.start())
    slope[...] = g * (1.0 + v * (1.0 - g))
    conv(0, fb, w1)

    for j in range(4):

        @pl.when(jnp.logical_not(mine & (slot == j)))
        def _():
            pltpu.make_async_copy(got_obs.at[j], got_obs.at[j], osem_r.at[0, j]).wait()
            pltpu.make_async_copy(got_noi.at[j], got_noi.at[j], osem_r.at[1, j]).wait()

    v = pc[...].reshape(384, 512) + cat([bias[1]] * 4, 1)
    g = gate(v)
    hidden = (v * g).astype(BF)
    predicted = nn(wp[...], hidden)
    seen = cat([got_obs[x].reshape(24, 128) for x in range(4)], 1)
    weight = cat([cat([got_noi[x]] * 3, 0) for x in range(4)], 1)
    residual = weight * (predicted - seen)
    high, low = split(residual)
    back = nn(wpt[...], high) + nn(wpt[...], low)
    grad_conv = (back * (g * (1.0 + v * (1.0 - g)))).astype(BF)
    fill(gb, grad_conv)
    halo(1, gb, lambda c: c.start())
    conv(1, gb, w2)
    grad_down = (pc[...].reshape(384, 512) * slope[...]).astype(BF)
    s5[...] = (stage_z_backward(t, nn(wbt[...], grad_down))).astype(s5.dtype)

    send_q(4, s5, r5)
    arrived(4, r5)
    s6[...] = (stage_y_backward(t, r5[...])).astype(s6.dtype)
    send_r(5, s6, r6)
    arrived(5, r6)
    s7[...] = (stage_x_backward(t, r6[...], fac[0], fac[2])).astype(s7.dtype)
    send_r(6, s7, r7)
    arrived(6, r7)
    s8[...] = (stage_y_final(t, r7[...])).astype(s8.dtype)
    send_q(7, s8, r8)
    for phase, ref in enumerate((s1, s2, s3, s4, s5, s6, s7)):
        sent(phase, ref)
    halo(0, fb, lambda c: c.wait_send())
    halo(1, gb, lambda c: c.wait_send())
    for j in range(4):

        @pl.when(jnp.logical_not(mine & (rem(q, 4) == j)))
        def _():
            observed_copies(j, lambda c: c.wait_send())

    arrived(7, r8)
    out[...] = stage_z_final(t, r8[...]).reshape(2, 64, 256)
    sent(7, s8)


def on_device(
    density, weight_down, bias_down, weight_conv, bias_conv, weight_out, observed, noise_precision
):
    vmem = pl.BlockSpec(memory_space=pltpu.VMEM)
    shapes = [(v.shape, BF) for v in TABLES.values()]
    inputs = (
        density,
        weight_down.T,
        bias_down.reshape(1, -1),
        weight_conv,
        bias_conv.reshape(1, -1),
        weight_out,
        observed,
        noise_precision,
    )
    shapes += [(v.shape, v.dtype) for v in inputs]
    wide, one = (16, 16, 128), (32, 8, 128)
    two, three = (32, 16, 128), (16, 3, 16, 128)
    for shape, kind in zip((wide, one, two, three, three, two, one, wide), KINDS):
        shapes += [(shape, kind)] * 2
    shapes += [
        ((6, 10, 48, 128), BF),
        ((6, 10, 48, 128), BF),
        ((10, 144, 768), BF),
        ((144, 432), BF),
        ((144, 432), BF),
        ((384, 192), BF),
        ((192, 384), BF),
        ((24, 384), BF),
        ((384, 24), BF),
        ((384, 512), F32),
        ((8, 48, 512), F32),
        ((4, 3, 8, 128), F32),
        ((4, 8, 128), F32),
        ((3, N, 128), F32),
        ((2, 384, 128), F32),
    ]
    dma = pltpu.SemaphoreType.DMA
    return pl.pallas_call(
        kernel,
        out_shape=jax.ShapeDtypeStruct((2, 64, 256), F32),
        in_specs=[pl.BlockSpec(memory_space=pltpu.HBM)] * (8 + len(NAMES)),
        out_specs=vmem,
        scratch_shapes=[pltpu.VMEM(shape, kind) for shape, kind in shapes]
        + [
            dma((len(NAMES),)),
            dma((8,)),
            dma((8,)),
            dma((8,)),
            dma((2, 8)),
            dma((2, 8)),
            dma((2, 4)),
            dma((2, 4)),
        ],
        compiler_params=pltpu.CompilerParams(
            collective_id=0, has_side_effects=True, vmem_limit_bytes=64 * 1024 * 1024
        ),
    )(
        *inputs,
        *[jnp.asarray(TABLES[name]) for name in NAMES],
    )


def solution(mesh):
    return jax.shard_map(
        on_device,
        mesh=mesh,
        in_specs=(
            P("slab", "pencil", None),
            P(),
            P(),
            P(),
            P(),
            P(),
            P(None, "slab", "pencil", None),
            P("slab", "pencil", None),
        ),
        out_specs=P("slab", "pencil", None),
        check_vma=False,
    )
```

```python
import functools

import jax
import jax.numpy as jnp
import ml_dtypes
import numpy as np
from jax import lax
from jax.experimental import pallas as pl
from jax.experimental.pallas import tpu as pltpu
from jax.sharding import PartitionSpec as P

MESH = pl.DeviceIdType.MESH
BF = jnp.bfloat16
F32 = jnp.float32
N = 256
GROWTH = 3.0
TWO_PI = 2.0 * np.pi
KINDS = (F32, F32, F32, F32, BF, F32, F32, F32)


def theta(a, b):
    return TWO_PI * ((a[:, None].astype(np.int64) * b[None, :]) % N) / N


def grid(*sizes):
    return [g.reshape(-1) for g in np.meshgrid(*[np.arange(s) for s in sizes], indexing="ij")]


def signed(k):
    return np.where(k < N // 2, k, k - N)


def wave(k):
    return np.where(k == N // 2, 0, signed(k)) * (TWO_PI / N)


def complex_rows(angle, c_out, c_in, sign, turn):
    value = np.exp(1j * sign * angle) * (1j**turn)
    a, b = c_out[:, None], c_in[None, :]
    same = a == b
    cross = np.where((a == 0) & (b == 1), -value.imag, value.imag)
    return np.where(same, value.real, cross)


def swap_rows(order_in, order_out, sign):
    rows_in = {key: i for i, key in enumerate(order_in)}
    count = len(order_in)
    out = np.zeros((2 * count, count))
    for i, key in enumerate(order_out):
        out[i, rows_in[key]] = 1.0
        name = dict(key)
        name["c"] = 1 - name["c"]
        other = tuple(name.items())
        out[count + i, rows_in[other]] = (1.0 if dict(key)["c"] == 0 else -1.0) * (-sign)
    return out


def keys(spec, canon):
    names = [n for n, _ in spec]
    axes = grid(*[s for _, s in spec])
    out = []
    for values in zip(*axes):
        d = dict(zip(names, (int(v) for v in values)))
        out.append(tuple((n, d[n]) for n in canon))
    return out


def tables():
    t = {}
    half = np.where(np.arange(N // 2) == 0, 1.0, 2.0) / float(N) ** 3
    z = np.arange(N)
    q, c, k = grid(16, 2, 8)
    kz = 8 * q + k
    t["zf"] = complex_rows(theta(kz, z), c, np.zeros(N, np.int64), -1, 0)
    par, zz = grid(2, 128)
    zc = 2 * zz + par
    back = complex_rows(theta(kz, zc), c, np.zeros(N, np.int64), -1, 0) * half[kz][:, None]
    t["zb"] = np.stack([back, back * wave(kz)[:, None]])
    q, k, c = grid(16, 8, 2)
    kz = 8 * q + k
    inv = complex_rows(theta(kz, zc).T, np.zeros(N, np.int64), c, 1, 0).T * half[kz][:, None]
    t["zi"] = np.stack([inv, inv * wave(kz)[:, None]])
    t["zj"] = complex_rows(theta(kz, z).T, np.zeros(N, np.int64), c, 1, 0).T
    a = np.arange(N)
    base = np.concatenate([np.cos(theta(a, a)), np.sin(theta(a, a))], axis=0)
    qy = wave(a)
    t["yt"] = base
    times = np.concatenate([qy, qy])[:, None] * base
    t["yi"] = times
    by = base * qy[None, :]
    t["yb"] = np.concatenate([by, base], axis=0)
    par, c_k, k2 = grid(2, 2, N // 2)
    kx = 2 * k2 + par
    r, w, c_in = grid(32, 4, 2)
    pos = lambda x1: 128 * (w // 2) + 4 * r + 2 * (w % 2) + x1
    t["xf"] = np.concatenate(
        [complex_rows(theta(kx, pos(v)), c_k, c_in, -1, 0) for v in (0, 1)], axis=0
    )
    t["xj"] = np.concatenate(
        [complex_rows(theta(kx, pos(v)).T, c_in, c_k, 1, -1) for v in (0, 1)], axis=0
    )
    c_h, k2 = grid(2, N // 2)
    r, c, x8 = grid(16, 2, 8)
    t["xi"] = np.stack(
        [complex_rows(theta(2 * k2 + p, 8 * r + x8).T, c, c_h, 1, 1) for p in (0, 1)]
    )
    r, x8, c = grid(16, 8, 2)
    t["xb"] = np.stack(
        [complex_rows(theta(2 * k2 + p, 8 * r + x8), c_h, c, -1, 0) for p in (0, 1)]
    )
    pairs = {}
    for name, value in t.items():
        high = value.astype(np.float32).astype(ml_dtypes.bfloat16)
        low = (value - high.astype(np.float64)).astype(np.float32).astype(ml_dtypes.bfloat16)
        pairs[name] = np.stack([high, low])
    canon = ("w", "c", "k")
    s = {}
    s["pf"] = swap_rows(
        keys((("w", 4), ("c", 2), ("k", 8)), canon), keys((("k", 8), ("w", 4), ("c", 2)), canon), -1
    )
    s["pj"] = swap_rows(
        keys((("k", 8), ("w", 4), ("c", 2)), canon), keys((("w", 4), ("k", 8), ("c", 2)), canon), 1
    )
    s["pi"] = swap_rows(
        keys((("k", 8), ("c", 2), ("w", 8)), canon), keys((("w", 8), ("k", 8), ("c", 2)), canon), 1
    )
    s["pb"] = swap_rows(
        keys((("w", 8), ("c", 2), ("k", 8)), canon), keys((("k", 8), ("w", 8), ("c", 2)), canon), -1
    )
    par, i, a, y = grid(2, 3, 2, 16)
    e2 = np.zeros((192, 24))
    e2[np.arange(192), 8 * i + 4 * a + 2 * (y % 2) + par] = 1.0
    s["e2t"] = e2
    e1 = np.zeros((384, 48))
    e1[np.arange(384), np.arange(384) % 48] = 1.0
    s["e1"] = e1
    for name, value in s.items():
        pairs[name] = value.astype(np.float32).astype(ml_dtypes.bfloat16)
    return pairs


def dot(a, b, ca, cb):
    return lax.dot_general(a, b, (((ca,), (cb,)), ((), ())), preferred_element_type=F32)


def nn(a, b):
    return dot(a, b, 1, 0)


def nt(a, b):
    return dot(a, b, 1, 1)


def tn(a, b):
    return dot(a, b, 0, 0)


def roll(x, shift):
    return pltpu.roll(x, shift % x.shape[-1], x.ndim - 1)


def split(x):
    high = x.astype(BF)
    return high, (x - high.astype(F32)).astype(BF)


def lanes():
    return lax.broadcasted_iota(jnp.int32, (1, 128), 1)


def low_halves(a, b):
    return jnp.where(lanes() < 64, a, roll(b, 64))


def high_halves(a, b):
    return jnp.where(lanes() < 64, roll(a, 64), b)


def transpose_groups(tiles):
    tiles = list(tiles)
    for d in (1, 2, 4):
        odd = (lanes() // (16 * d)) % 2 == 1
        for i in range(8):
            if i & d:
                continue
            low, high = tiles[i], tiles[i + d]
            tiles[i] = jnp.where(odd, roll(high, 16 * d), low)
            tiles[i + d] = jnp.where(odd, high, roll(low, 128 - 16 * d))
    return tiles


def cat(parts, axis):
    return jnp.concatenate(list(parts), axis=axis)


def parts_of(x, kind):
    return (x.astype(BF),) if kind == BF else split(x)


def pair_swapped(moved, rows, fields):
    return [
        cat([moved[:rows, 256 * f : 256 * f + 256], moved[rows:, 256 * f : 256 * f + 256]], 1)
        for f in range(fields)
    ]


def table_left(form, t, x, index=()):
    high, low = t[(0, *index)], t[(1, *index)]
    out = form(high, x[0]) + form(low, x[0])
    if len(x) > 1:
        out = out + form(high, x[1])
    return out


def table_right(form, x, t, index=()):
    high, low = t[(0, *index)], t[(1, *index)]
    out = form(x[0], high) + form(x[0], low)
    if len(x) > 1:
        out = out + form(x[1], high)
    return out


def stage_z_forward(t, density):
    return table_left(nt, t["zf"], split(density)).reshape(16, 16, 128)


def stage_y_forward(t, got):
    z_rows = [got[4 * i : 4 * i + 4].reshape(64, 128).astype(F32) for i in range(4)]
    x = cat(
        [f(z_rows[2 * a], z_rows[2 * a + 1]) for f in (low_halves, high_halves) for a in (0, 1)], 1
    )
    left = [
        cat(pair_swapped(nn(t["pf"][...], part).astype(BF), 64, 2), 0)
        for part in parts_of(x, got.dtype)
    ]
    out = table_right(nn, left, t["yt"])
    first, second = out[:64], out[64:]
    parts = []
    for a in (0, 1):
        u, v = first[:, 128 * a : 128 * a + 128], second[:, 128 * a : 128 * a + 128]
        parts += [low_halves(u, v), high_halves(u, v)]
    return jnp.stack([p.reshape(8, 8, 128) for p in parts], axis=1).reshape(32, 8, 128)


def factors(q, r):
    kz = 8 * q + r // 4
    row = lax.broadcasted_iota(jnp.int32, (N, 128), 0)
    lane = lax.broadcasted_iota(jnp.int32, (N, 128), 1)
    ky = 64 * (r % 4) + lane % 64
    spacing = F32(TWO_PI / N)

    kx = 2 * (row % 128) + row // 128

    def full(k):
        return jnp.where(k < N // 2, k, k - N).astype(F32) * spacing

    fx, fy = full(kx), full(ky)
    fz = (kz + 0 * row).astype(F32) * spacing
    square = fx * fx + fy * fy + fz * fz
    anchor = (kx == 0) & (ky == 0) & (kz == 0)
    square = jnp.where(anchor, F32(1.0), square)
    qx = jnp.where(kx == N // 2, F32(0.0), fx)
    first = lane < 64
    inverse = F32(GROWTH) / square
    return inverse, jnp.where(first, inverse, inverse * qx), jnp.where(first, qx, F32(1.0))


def times_rows(x, factor):
    half = N // 2
    return (x.reshape(2, 2, half, 128) * factor.reshape(2, 1, half, 128)).reshape(2 * N, 128)


def stage_x_forward(t, got, factor):
    y = table_left(nn, t["xf"], split(got.reshape(256, 128)))
    z = jnp.where(lanes() < 64, y[:512], y[512:])
    modes = times_rows(z + roll(z, 64), factor)
    even = table_left(nn, t["xi"], split(modes[:256]), (0,))
    odd = table_left(nn, t["xi"], split(modes[256:]), (1,))
    return cat([even + odd, even - odd], 0).reshape(32, 16, 128)


def stage_y_inverse(t, got):
    kind = got.dtype
    got = got.reshape(8, 4, 16, 128)
    tile = [got[:, i].reshape(128, 128).astype(F32) for i in range(4)]
    x = cat([f(tile[2 * a], tile[2 * a + 1]) for f in (low_halves, high_halves) for a in (0, 1)], 1)
    return [pair_swapped(nn(t["pi"][...], part).astype(BF), 128, 2) for part in parts_of(x, kind)]


def y_inverse_field(t, left, i):
    field = table_right(
        nn, [p[1 if i == 0 else 0] for p in left], t["yi" if i == 1 else "yt"]
    )
    tiles = transpose_groups(
        cat([field[16 * k : 16 * k + 16, 128 * h : 128 * h + 128] for h in (0, 1)], 0)
        for k in range(8)
    )
    return jnp.stack([tiles[k][16 * h : 16 * h + 16] for h in (0, 1) for k in range(8)], axis=0)


def z_inverse_field(t, got, i):
    m = parts_of(got.reshape(256, 128), got.dtype)
    return table_right(tn, m, t["zi"], (1 if i == 2 else 0,)).astype(BF)


def block_cells(psi):
    rows = []
    for par in (0, 1):
        for i in range(3):
            for a in (0, 1):
                rows.append(
                    cat(
                        [
                            psi[i][32 * x + 16 * a : 32 * x + 16 * a + 16, 128 * par : 128 * par + 128]
                            for x in range(4)
                        ],
                        1,
                    )
                )
    return cat(rows, 0)


def stage_z_backward(t, grad):
    out = []
    for i in range(3):
        block = []
        for x in range(4):
            for a in (0, 1):
                block.append(
                    cat(
                        [
                            grad[
                                16 * (6 * par + 2 * i + a) : 16 * (6 * par + 2 * i + a) + 16,
                                128 * x : 128 * x + 128,
                            ]
                            for par in (0, 1)
                        ],
                        1,
                    )
                )
        field = cat(block, 0)
        o = table_left(nt, t["zb"], split(field), (1 if i == 2 else 0,))
        out.append(o.reshape(16, 16, 128))
    return jnp.stack(out, axis=1)


def stage_y_backward(t, got):
    tiles = [
        cat([got[8 * h + i, f] for f in range(3) for h in (0, 1)], 0).astype(F32) for i in range(8)
    ]
    tiles = transpose_groups(tiles)
    x = cat(
        [
            cat([tiles[i][16 * (2 * f + h) : 16 * (2 * f + h) + 16] for i in range(8)], 0)
            for f in range(3)
            for h in (0, 1)
        ],
        1,
    )
    pairs = [
        pair_swapped(nn(t["pb"][...], part).astype(BF), 128, 3) for part in parts_of(x, got.dtype)
    ]
    gx = table_right(nn, [p[0] for p in pairs], t["yt"])
    rest = table_right(nn, [cat(p[1:], 1) for p in pairs], t["yb"])
    parts = []
    for a in (0, 1):
        u, v = gx[:, 128 * a : 128 * a + 128], rest[:, 128 * a : 128 * a + 128]
        parts += [low_halves(u, v), high_halves(u, v)]
    return jnp.stack([p.reshape(8, 16, 128) for p in parts], axis=1).reshape(32, 16, 128)


def stage_x_backward(t, got, inverse, along):
    planes = got.reshape(512, 128).astype(F32)
    low, high = planes[:256], planes[256:]
    even = table_left(nn, t["xb"], split(low + high), (0,))
    odd = table_left(nn, t["xb"], split(low - high), (1,))
    y = times_rows(cat([even, odd], 0), along)
    modes = times_rows(y + roll(y, 64), inverse)
    o = table_left(nn, t["xj"], split(modes))
    return jnp.where(lanes() < 64, o[:256], o[256:]).reshape(32, 8, 128)


def stage_y_final(t, got):
    kind = got.dtype
    got = got.reshape(8, 4, 8, 128)
    tile = [got[:, i].reshape(64, 128) for i in range(4)]
    x = cat([f(tile[2 * a], tile[2 * a + 1]) for f in (low_halves, high_halves) for a in (0, 1)], 1)
    lefts = [
        cat(pair_swapped(nn(t["pj"][...], part).astype(BF), 64, 2), 0)
        for part in parts_of(x, kind)
    ]
    out = table_right(nn, lefts, t["yt"])
    first, second = out[:64], out[64:]
    parts = []
    for a in (0, 1):
        u, v = first[:, 128 * a : 128 * a + 128], second[:, 128 * a : 128 * a + 128]
        parts += [low_halves(u, v), high_halves(u, v)]
    return cat([p.reshape(4, 16, 128) for p in parts], 0)


def stage_z_final(t, got):
    return table_right(tn, parts_of(got.reshape(256, 128), got.dtype), t["zj"])


def iota2(shape, dim):
    return lax.broadcasted_iota(jnp.int32, shape, dim)


def down_weights(t, wd):
    eight = nt(t["e1"][...], wd).astype(BF)
    row, col = iota2((384, 192), 0), iota2((384, 192), 1)
    w = jnp.where(row // 48 == (col % 16) // 2, nt(eight, t["e2t"][...]), 0.0).astype(BF)
    row, col = iota2((192, 384), 0), iota2((192, 384), 1)
    wt = jnp.where(col // 48 == (row % 16) // 2, nt(t["e2t"][...], eight), 0.0).astype(BF)
    return w, wt


def out_weights(t, wo):
    wide = wo.astype(F32)
    each = cat([jnp.broadcast_to(wide[j : j + 1], (8, 48)) for j in range(3)], 0).astype(BF)
    row, col = iota2((24, 384), 0), iota2((24, 384), 1)
    w = jnp.where(row % 8 == col // 48, nt(each, t["e1"][...]), 0.0).astype(BF)
    row, col = iota2((384, 24), 0), iota2((384, 24), 1)
    wt = jnp.where(row // 48 == col % 8, nt(t["e1"][...], each), 0.0).astype(BF)
    return w, wt


def bias_rows(t, b):
    out, left = 0.0, b
    for _ in range(3):
        part = left.astype(BF)
        out = out + nt(t["e1"][...], jnp.broadcast_to(part.astype(F32), (128, 48)).astype(BF))
        left = left - part.astype(F32)
    return out


def place(i):
    return (iota2((48, 432), 1) == 48 * i + iota2((48, 432), 0)).astype(F32).astype(BF)


def conv_weights(wc):
    out = 0.0
    for i in range(9):
        out = out + nn(cat([wc[9 * dx + i] for dx in range(3)], 0), place(i))
    return out.astype(BF)


def conv_weights_back(wc):
    rows = []
    for ex in range(3):
        out = 0.0
        for i in range(9):
            out = out + tn(wc[26 - 9 * ex - i], place(i))
        rows.append(out)
    return cat(rows, 0).astype(BF)


def add_taps(o):
    return o[:48, :512] + o[48:96, 128:640] + o[96:, 256:]


def add_own_taps(o):
    none = jnp.zeros((48, 128), F32)
    return o[48:96] + cat([none, o[:48, :384]], 1) + cat([o[96:, 128:], none], 1)


def gate(v):
    return 0.5 + 0.5 * jnp.tanh(0.5 * v)


TABLES = tables()
NAMES = tuple(TABLES)


Q_AHEAD = sorted(
    [(dz, dc) for dz in range(8) for dc in range(2) if dz or dc],
    key=lambda t: -(min(t[0], 8 - t[0]) + 0.3 * t[1]),
)
R_AHEAD = sorted(
    [(dx, dy) for dx in range(4) for dy in range(8) if dx or dy],
    key=lambda t: -(min(t[0], 4 - t[0]) + min(t[1], 8 - t[1])),
)
rem = lax.rem
div = lax.div


def kernel(*refs):
    args = refs[:8]
    count = len(NAMES)
    source = dict(zip(NAMES, refs[8 : 8 + count]))
    out = refs[8 + count]
    rest = refs[9 + count :]
    t = dict(zip(NAMES, rest[:count]))
    rest = rest[count:]
    here, rest = rest[:8], rest[8:]
    den, wd, bd, wc, bc, wo, obs, noi = here
    (s1, r1, s2, r2, s3, r3, s4, r4, s5, r5, s6, r6, s7, r7, s8, r8) = rest[:16]
    (fb, gb, sb, w1, w2, wb, wbt, wp, wpt, slope, pc, got_obs, got_noi, fac, bias) = rest[16:31]
    tsem, asem, ssem, rsem, hsem_s, hsem_r, osem_s, osem_r = rest[31:]

    s = lax.axis_index("slab")
    zh = lax.axis_index("pencil")
    core = rem(s, 2)
    r = rem(div(s, 2), 32)
    zl = div(s, 64)
    z = 2 * zh + zl
    q = 2 * z + core
    rx, ry = div(r, 8), rem(r, 8)

    def device(q, r):
        return {"slab": 64 * rem(div(q, 2), 2) + 2 * r + rem(q, 2), "pencil": div(q, 4)}

    def q_partners():
        for dz, dc in Q_AHEAD:
            z2 = rem(z + dz, 8) if dz else z
            c2 = 1 - core if dc else core
            yield (
                2 * z2 + c2,
                {"slab": 64 * rem(z2, 2) + 2 * r + c2, "pencil": div(z2, 2)},
            )

    def r_partners():
        for dx, dy in R_AHEAD:
            x2 = rem(rx + dx, 4) if dx else rx
            y2 = rem(ry + dy, 8) if dy else ry
            r2 = 8 * x2 + y2
            yield r2, {"slab": 64 * zl + 2 * r2 + core, "pencil": zh}

    first = NAMES.index("zf")

    def load(i):
        pltpu.make_async_copy(args[i], here[i], asem.at[i]).start()

    def load_table(i):
        pltpu.make_async_copy(source[NAMES[i]], t[NAMES[i]], tsem.at[i]).start()

    load(0)
    load_table(first)

    barrier = pltpu.get_barrier_semaphore()

    def greet(dev):
        pl.semaphore_signal(barrier, inc=1, device_id=dev, device_id_type=MESH)

    for _, dev in r_partners():
        greet(dev)
    for _, dev in q_partners():
        greet(dev)
    for dq in (1, 15):
        for dr in (1, 31):
            greet(device(rem(q + dq, 16), rem(r + dr, 32)))
    home = div(s, 4)
    slot = rem(s, 4)
    mine = home == r
    own = mine.astype(jnp.int32)
    for j in range(4):

        @pl.when(jnp.logical_not(mine & (rem(q, 4) == j)))
        def _():
            greet(device(4 * zh + j, home))

        @pl.when(jnp.logical_not(mine & (slot == j)))
        def _():
            greet({"slab": 4 * r + j, "pencil": zh})

    for i in (6, 7, *range(1, 6)):
        load(i)
    for i in range(len(NAMES)):
        if i != first:
            load_table(i)

    def ready(*names):
        for name in names:
            pltpu.make_async_copy(source[name], t[name], tsem.at[NAMES.index(name)]).wait()

    def have(*numbers):
        for i in numbers:
            pltpu.make_async_copy(args[i], here[i], asem.at[i]).wait()

    def send(phase, src, dst, me, partners):
        for d, dev in partners:
            pltpu.make_async_remote_copy(
                src_ref=src.at[d],
                dst_ref=dst.at[me],
                send_sem=ssem.at[phase],
                recv_sem=rsem.at[phase],
                device_id=dev,
                device_id_type=MESH,
            ).start()
        dst[me] = src[me]

    def send_q(phase, src, dst):
        send(phase, src, dst, q, q_partners())

    def send_r(phase, src, dst):
        send(phase, src, dst, r, r_partners())

    def arrived(phase, dst):
        part = dst.at[pl.ds(0, dst.shape[0] - 1)]
        pltpu.make_async_copy(part, part, rsem.at[phase]).wait()

    def sent(phase, src):
        part = src.at[pl.ds(0, src.shape[0] - 1)]
        pltpu.make_async_copy(part, part, ssem.at[phase]).wait()

    def halo(which, buf, action):
        cut = {0: ((1, 5), (1, 5)), 1: ((4, 5), (0, 1)), -1: ((1, 2), (5, 6))}
        line = {0: ((1, 9), (1, 9)), 1: ((8, 9), (0, 1)), -1: ((1, 2), (9, 10))}
        ways = ((1, 0), (-1, 0), (1, 1), (1, -1), (-1, 1), (-1, -1), (0, 1), (0, -1))
        for k, (dr, dq) in enumerate(ways):
            (a, b), (c, d) = cut[dr]
            (e, f), (g, h) = line[dq]
            copy = pltpu.make_async_remote_copy(
                src_ref=buf.at[pl.ds(a, b - a), pl.ds(e, f - e)],
                dst_ref=buf.at[pl.ds(c, d - c), pl.ds(g, h - g)],
                send_sem=hsem_s.at[which, k],
                recv_sem=hsem_r.at[which, k],
                device_id=device(rem(q + dq + 16, 16), rem(r + dr + 32, 32)),
                device_id_type=MESH,
            )
            action(copy)

    def shifted(buf, rows, tiles):
        lo, hi = rows
        for x in tiles:
            part = buf[x, lo:hi].reshape(48 * (hi - lo), 128)
            for dz, value in enumerate((roll(part, 1), part, roll(part, 127))):
                sb[lo:hi, 48 * dz : 48 * dz + 48, 128 * x : 128 * x + 128] = value.reshape(
                    hi - lo, 48, 128
                )

    def fill(buf, value):
        for x in range(4):
            buf[x + 1, 1:9] = value[:, 128 * x : 128 * x + 128].reshape(8, 48, 128)

    def conv(which, buf, weights):
        shifted(buf, (1, 9), range(1, 5))

        def inner(y, carry):
            o = nn(weights[...], sb[pl.ds(y, 3), :, 128:640].reshape(432, 512))
            pc[y] = add_own_taps(o)
            return carry

        lax.fori_loop(1, 7, inner, 0)
        halo(which, buf, lambda c: c.wait_recv())
        shifted(buf, (0, 10), (0, 5))
        shifted(buf, (0, 1), range(1, 5))
        shifted(buf, (9, 10), range(1, 5))

        def edges(y, carry):
            side = cat([sb[pl.ds(y, 3), :, 0:128], sb[pl.ds(y, 3), :, 640:768]], 2)
            o = nn(weights[...], side.reshape(432, 256))
            pc[y, :, 0:128] += o[:48, :128]
            pc[y, :, 384:512] += o[96:, 128:]
            return carry

        lax.fori_loop(1, 7, edges, 0)
        for y in (0, 7):
            pc[y] = add_taps(nn(weights[...], sb[y : y + 3].reshape(432, 768)))

    have(0)
    ready("zf")
    s1[...] = (stage_z_forward(t, den[...].reshape(128, 256))).astype(s1.dtype)
    have(6, 7)
    pl.semaphore_wait(barrier, 58 - 2 * own)
    send_q(0, s1, r1)

    def observed_copies(j, action):
        for src, dst, kind in (
            (obs.at[:, 0, pl.ds(8 * j, 8), :], got_obs.at[slot], 0),
            (noi.at[0, pl.ds(8 * j, 8), :], got_noi.at[slot], 1),
        ):
            action(
                pltpu.make_async_remote_copy(
                    src_ref=src,
                    dst_ref=dst,
                    send_sem=osem_s.at[kind, j],
                    recv_sem=osem_r.at[kind, slot],
                    device_id=device(4 * zh + j, home),
                    device_id_type=MESH,
                )
            )

    for j in range(4):
        this = mine & (rem(q, 4) == j)

        @pl.when(jnp.logical_not(this))
        def _():
            observed_copies(j, lambda c: c.start())

        @pl.when(this)
        def _():
            got_obs[slot] = obs[:, 0, 8 * j : 8 * j + 8, :]
            got_noi[slot] = noi[0, 8 * j : 8 * j + 8, :]

    inverse, both, along = factors(q, r)
    fac[0] = inverse
    fac[1] = both
    fac[2] = along
    ready("e1", "e2t")
    have(1, 2, 3, 4, 5)
    w, wt = down_weights(t, wd[...])
    wb[...] = w
    wbt[...] = wt
    w, wt = out_weights(t, wo[...])
    wp[...] = w
    wpt[...] = wt
    bias[0] = bias_rows(t, bd[...])
    bias[1] = bias_rows(t, bc[...])

    arrived(0, r1)
    ready("pf", "yt")
    s2[...] = (stage_y_forward(t, r1[...])).astype(s2.dtype)
    send_r(1, s2, r2)
    w1[...] = conv_weights(wc)
    arrived(1, r2)
    ready("xf", "xi")
    s3[...] = (stage_x_forward(t, r2[...], fac[1])).astype(s3.dtype)
    send_r(2, s3, r3)
    w2[...] = conv_weights_back(wc)
    arrived(2, r3)
    ready("pi", "yi")
    left = stage_y_inverse(t, r3[...])
    for i in range(3):
        s4[i] = y_inverse_field(t, left, i).astype(s4.dtype)
        send_q((3, 8, 9)[i], s4.at[i], r4.at[i])
    ready("zi", "zb", "pb", "yb", "xb", "xj", "pj", "zj")

    psi = []
    for i in range(3):
        arrived((3, 8, 9)[i], r4.at[i])
        psi.append(z_inverse_field(t, r4[i], i))
    cells = block_cells(psi)
    v = nn(wb[...], cells) + cat([bias[0]] * 4, 1)
    g = gate(v)
    fill(fb, (v * g).astype(BF))
    halo(0, fb, lambda c: c.start())
    slope[...] = g * (1.0 + v * (1.0 - g))
    conv(0, fb, w1)

    for j in range(4):

        @pl.when(jnp.logical_not(mine & (slot == j)))
        def _():
            pltpu.make_async_copy(got_obs.at[j], got_obs.at[j], osem_r.at[0, j]).wait()
            pltpu.make_async_copy(got_noi.at[j], got_noi.at[j], osem_r.at[1, j]).wait()

    v = pc[...].reshape(384, 512) + cat([bias[1]] * 4, 1)
    g = gate(v)
    hidden = (v * g).astype(BF)
    predicted = nn(wp[...], hidden)
    seen = cat([got_obs[x].reshape(24, 128) for x in range(4)], 1)
    weight = cat([cat([got_noi[x]] * 3, 0) for x in range(4)], 1)
    residual = weight * (predicted - seen)
    high, low = split(residual)
    back = nn(wpt[...], high) + nn(wpt[...], low)
    grad_conv = (back * (g * (1.0 + v * (1.0 - g)))).astype(BF)
    fill(gb, grad_conv)
    halo(1, gb, lambda c: c.start())
    conv(1, gb, w2)
    grad_down = (pc[...].reshape(384, 512) * slope[...]).astype(BF)
    s5[...] = (stage_z_backward(t, nn(wbt[...], grad_down))).astype(s5.dtype)

    send_q(4, s5, r5)
    arrived(4, r5)
    s6[...] = (stage_y_backward(t, r5[...])).astype(s6.dtype)
    send_r(5, s6, r6)
    arrived(5, r6)
    s7[...] = (stage_x_backward(t, r6[...], fac[0], fac[2])).astype(s7.dtype)
    send_r(6, s7, r7)
    arrived(6, r7)
    s8[...] = (stage_y_final(t, r7[...])).astype(s8.dtype)
    send_q(7, s8, r8)
    for phase, ref in zip((0, 1, 2, 4, 5, 6), (s1, s2, s3, s5, s6, s7)):
        sent(phase, ref)
    for i in range(3):
        sent((3, 8, 9)[i], s4.at[i])
    halo(0, fb, lambda c: c.wait_send())
    halo(1, gb, lambda c: c.wait_send())
    for j in range(4):

        @pl.when(jnp.logical_not(mine & (rem(q, 4) == j)))
        def _():
            observed_copies(j, lambda c: c.wait_send())

    arrived(7, r8)
    out[...] = stage_z_final(t, r8[...]).reshape(2, 64, 256)
    sent(7, s8)


def on_device(
    density, weight_down, bias_down, weight_conv, bias_conv, weight_out, observed, noise_precision
):
    vmem = pl.BlockSpec(memory_space=pltpu.VMEM)
    shapes = [(v.shape, BF) for v in TABLES.values()]
    inputs = (
        density,
        weight_down.T,
        bias_down.reshape(1, -1),
        weight_conv,
        bias_conv.reshape(1, -1),
        weight_out,
        observed,
        noise_precision,
    )
    shapes += [(v.shape, v.dtype) for v in inputs]
    wide, one = (16, 16, 128), (32, 8, 128)
    two, three, apart = (32, 16, 128), (16, 3, 16, 128), (3, 16, 16, 128)
    for shape, kind in zip((wide, one, two, apart, three, two, one, wide), KINDS):
        shapes += [(shape, kind)] * 2
    shapes += [
        ((6, 10, 48, 128), BF),
        ((6, 10, 48, 128), BF),
        ((10, 144, 768), BF),
        ((144, 432), BF),
        ((144, 432), BF),
        ((384, 192), BF),
        ((192, 384), BF),
        ((24, 384), BF),
        ((384, 24), BF),
        ((384, 512), F32),
        ((8, 48, 512), F32),
        ((4, 3, 8, 128), F32),
        ((4, 8, 128), F32),
        ((3, N, 128), F32),
        ((2, 384, 128), F32),
    ]
    dma = pltpu.SemaphoreType.DMA
    return pl.pallas_call(
        kernel,
        out_shape=jax.ShapeDtypeStruct((2, 64, 256), F32),
        in_specs=[pl.BlockSpec(memory_space=pltpu.HBM)] * (8 + len(NAMES)),
        out_specs=vmem,
        scratch_shapes=[pltpu.VMEM(shape, kind) for shape, kind in shapes]
        + [
            dma((len(NAMES),)),
            dma((8,)),
            dma((10,)),
            dma((10,)),
            dma((2, 8)),
            dma((2, 8)),
            dma((2, 4)),
            dma((2, 4)),
        ],
        compiler_params=pltpu.CompilerParams(
            collective_id=0, has_side_effects=True, vmem_limit_bytes=50 * 1024 * 1024
        ),
    )(
        *[pltpu.with_memory_space_constraint(v, pltpu.HBM) for v in inputs],
        *[pltpu.with_memory_space_constraint(jnp.asarray(TABLES[name]), pltpu.HBM) for name in NAMES],
    )


def solution(mesh):
    return jax.shard_map(
        on_device,
        mesh=mesh,
        in_specs=(
            P("slab", "pencil", None),
            P(),
            P(),
            P(),
            P(),
            P(),
            P(None, "slab", "pencil", None),
            P("slab", "pencil", None),
        ),
        out_specs=P("slab", "pencil", None),
        check_vma=False,
    )
```

```python
import functools

import jax
import jax.numpy as jnp
import ml_dtypes
import numpy as np
from jax import lax
from jax.experimental import pallas as pl
from jax.experimental.pallas import tpu as pltpu
from jax.sharding import PartitionSpec as P

MESH = pl.DeviceIdType.MESH
BF = jnp.bfloat16
F32 = jnp.float32
N = 256
GROWTH = 3.0
TWO_PI = 2.0 * np.pi
KINDS = (F32, F32, F32, F32, BF, F32, F32, F32)


def theta(a, b):
    return TWO_PI * ((a[:, None].astype(np.int64) * b[None, :]) % N) / N


def grid(*sizes):
    return [g.reshape(-1) for g in np.meshgrid(*[np.arange(s) for s in sizes], indexing="ij")]


def signed(k):
    return np.where(k < N // 2, k, k - N)


def wave(k):
    return np.where(k == N // 2, 0, signed(k)) * (TWO_PI / N)


def complex_rows(angle, c_out, c_in, sign, turn):
    value = np.exp(1j * sign * angle) * (1j**turn)
    a, b = c_out[:, None], c_in[None, :]
    same = a == b
    cross = np.where((a == 0) & (b == 1), -value.imag, value.imag)
    return np.where(same, value.real, cross)


def swap_rows(order_in, order_out, sign):
    rows_in = {key: i for i, key in enumerate(order_in)}
    count = len(order_in)
    out = np.zeros((2 * count, count))
    for i, key in enumerate(order_out):
        out[i, rows_in[key]] = 1.0
        name = dict(key)
        name["c"] = 1 - name["c"]
        other = tuple(name.items())
        out[count + i, rows_in[other]] = (1.0 if dict(key)["c"] == 0 else -1.0) * (-sign)
    return out


def keys(spec, canon):
    names = [n for n, _ in spec]
    axes = grid(*[s for _, s in spec])
    out = []
    for values in zip(*axes):
        d = dict(zip(names, (int(v) for v in values)))
        out.append(tuple((n, d[n]) for n in canon))
    return out


def tables():
    t = {}
    half = np.where(np.arange(N // 2) == 0, 1.0, 2.0) / float(N) ** 3
    z = np.arange(N)
    q, c, k = grid(16, 2, 8)
    kz = 8 * q + k
    t["zf"] = complex_rows(theta(kz, z), c, np.zeros(N, np.int64), -1, 0)
    par, zz = grid(2, 128)
    zc = 2 * zz + par
    back = complex_rows(theta(kz, zc), c, np.zeros(N, np.int64), -1, 0) * half[kz][:, None]
    t["zb"] = np.stack([back, back * wave(kz)[:, None]])
    q, k, c = grid(16, 8, 2)
    kz = 8 * q + k
    inv = complex_rows(theta(kz, zc).T, np.zeros(N, np.int64), c, 1, 0).T * half[kz][:, None]
    t["zi"] = np.stack([inv, inv * wave(kz)[:, None]])
    t["zj"] = complex_rows(theta(kz, z).T, np.zeros(N, np.int64), c, 1, 0).T
    a = np.arange(N)
    base = np.concatenate([np.cos(theta(a, a)), np.sin(theta(a, a))], axis=0)
    qy = wave(a)
    t["yt"] = base
    times = np.concatenate([qy, qy])[:, None] * base
    t["yi"] = times
    by = base * qy[None, :]
    t["yb"] = np.concatenate([by, base], axis=0)
    par, c_k, k2 = grid(2, 2, N // 2)
    kx = 2 * k2 + par
    r, w, c_in = grid(32, 4, 2)
    pos = lambda x1: 128 * (w // 2) + 4 * r + 2 * (w % 2) + x1
    t["xf"] = np.concatenate(
        [complex_rows(theta(kx, pos(v)), c_k, c_in, -1, 0) for v in (0, 1)], axis=0
    )
    t["xj"] = np.concatenate(
        [complex_rows(theta(kx, pos(v)).T, c_in, c_k, 1, -1) for v in (0, 1)], axis=0
    )
    c_h, k2 = grid(2, N // 2)
    r, c, x8 = grid(16, 2, 8)
    t["xi"] = np.stack(
        [complex_rows(theta(2 * k2 + p, 8 * r + x8).T, c, c_h, 1, 1) for p in (0, 1)]
    )
    r, x8, c = grid(16, 8, 2)
    t["xb"] = np.stack(
        [complex_rows(theta(2 * k2 + p, 8 * r + x8), c_h, c, -1, 0) for p in (0, 1)]
    )
    pairs = {}
    for name, value in t.items():
        high = value.astype(np.float32).astype(ml_dtypes.bfloat16)
        low = (value - high.astype(np.float64)).astype(np.float32).astype(ml_dtypes.bfloat16)
        pairs[name] = np.stack([high, low])
    canon = ("w", "c", "k")
    s = {}
    s["pf"] = swap_rows(
        keys((("w", 4), ("c", 2), ("k", 8)), canon), keys((("k", 8), ("w", 4), ("c", 2)), canon), -1
    )
    s["pj"] = swap_rows(
        keys((("k", 8), ("w", 4), ("c", 2)), canon), keys((("w", 4), ("k", 8), ("c", 2)), canon), 1
    )
    s["pi"] = swap_rows(
        keys((("k", 8), ("c", 2), ("w", 8)), canon), keys((("w", 8), ("k", 8), ("c", 2)), canon), 1
    )
    s["pb"] = swap_rows(
        keys((("w", 8), ("c", 2), ("k", 8)), canon), keys((("k", 8), ("w", 8), ("c", 2)), canon), -1
    )
    par, i, a, y = grid(2, 3, 2, 16)
    e2 = np.zeros((192, 24))
    e2[np.arange(192), 8 * i + 4 * a + 2 * (y % 2) + par] = 1.0
    s["e2t"] = e2
    e1 = np.zeros((384, 48))
    e1[np.arange(384), np.arange(384) % 48] = 1.0
    s["e1"] = e1
    for name, value in s.items():
        pairs[name] = value.astype(np.float32).astype(ml_dtypes.bfloat16)
    return pairs


def dot(a, b, ca, cb):
    return lax.dot_general(a, b, (((ca,), (cb,)), ((), ())), preferred_element_type=F32)


def nn(a, b):
    return dot(a, b, 1, 0)


def nt(a, b):
    return dot(a, b, 1, 1)


def tn(a, b):
    return dot(a, b, 0, 0)


def roll(x, shift):
    return pltpu.roll(x, shift % x.shape[-1], x.ndim - 1)


def split(x):
    high = x.astype(BF)
    return high, (x - high.astype(F32)).astype(BF)


def lanes():
    return lax.broadcasted_iota(jnp.int32, (1, 128), 1)


def low_halves(a, b):
    return jnp.where(lanes() < 64, a, roll(b, 64))


def high_halves(a, b):
    return jnp.where(lanes() < 64, roll(a, 64), b)


def transpose_groups(tiles):
    tiles = list(tiles)
    for d in (1, 2, 4):
        odd = (lanes() // (16 * d)) % 2 == 1
        for i in range(8):
            if i & d:
                continue
            low, high = tiles[i], tiles[i + d]
            tiles[i] = jnp.where(odd, roll(high, 16 * d), low)
            tiles[i + d] = jnp.where(odd, high, roll(low, 128 - 16 * d))
    return tiles


def cat(parts, axis):
    return jnp.concatenate(list(parts), axis=axis)


def parts_of(x, kind):
    return (x.astype(BF),) if kind == BF else split(x)


def pair_swapped(moved, rows, fields):
    return [
        cat([moved[:rows, 256 * f : 256 * f + 256], moved[rows:, 256 * f : 256 * f + 256]], 1)
        for f in range(fields)
    ]


def table_left(form, t, x, index=()):
    high, low = t[(0, *index)], t[(1, *index)]
    out = form(high, x[0]) + form(low, x[0])
    if len(x) > 1:
        out = out + form(high, x[1])
    return out


def table_right(form, x, t, index=()):
    high, low = t[(0, *index)], t[(1, *index)]
    out = form(x[0], high) + form(x[0], low)
    if len(x) > 1:
        out = out + form(x[1], high)
    return out


def stage_z_forward(t, density):
    return table_left(nt, t["zf"], split(density)).reshape(16, 16, 128)


def stage_y_forward(t, got):
    z_rows = [got[4 * i : 4 * i + 4].reshape(64, 128).astype(F32) for i in range(4)]
    x = cat(
        [f(z_rows[2 * a], z_rows[2 * a + 1]) for f in (low_halves, high_halves) for a in (0, 1)], 1
    )
    left = [
        cat(pair_swapped(nn(t["pf"][...], part).astype(BF), 64, 2), 0)
        for part in parts_of(x, got.dtype)
    ]
    out = table_right(nn, left, t["yt"])
    first, second = out[:64], out[64:]
    parts = []
    for a in (0, 1):
        u, v = first[:, 128 * a : 128 * a + 128], second[:, 128 * a : 128 * a + 128]
        parts += [low_halves(u, v), high_halves(u, v)]
    return jnp.stack([p.reshape(8, 8, 128) for p in parts], axis=1).reshape(32, 8, 128)


def factors(q, r):
    kz = 8 * q + r // 4
    row = lax.broadcasted_iota(jnp.int32, (N, 128), 0)
    lane = lax.broadcasted_iota(jnp.int32, (N, 128), 1)
    ky = 64 * (r % 4) + lane % 64
    spacing = F32(TWO_PI / N)

    kx = 2 * (row % 128) + row // 128

    def full(k):
        return jnp.where(k < N // 2, k, k - N).astype(F32) * spacing

    fx, fy = full(kx), full(ky)
    fz = (kz + 0 * row).astype(F32) * spacing
    square = fx * fx + fy * fy + fz * fz
    anchor = (kx == 0) & (ky == 0) & (kz == 0)
    square = jnp.where(anchor, F32(1.0), square)
    qx = jnp.where(kx == N // 2, F32(0.0), fx)
    first = lane < 64
    inverse = F32(GROWTH) / square
    return inverse, jnp.where(first, inverse, inverse * qx), jnp.where(first, qx, F32(1.0))


def times_rows(x, factor):
    half = N // 2
    return (x.reshape(2, 2, half, 128) * factor.reshape(2, 1, half, 128)).reshape(2 * N, 128)


def stage_x_forward(t, got, factor):
    y = table_left(nn, t["xf"], split(got.reshape(256, 128)))
    z = jnp.where(lanes() < 64, y[:512], y[512:])
    modes = times_rows(z + roll(z, 64), factor)
    even = table_left(nn, t["xi"], split(modes[:256]), (0,))
    odd = table_left(nn, t["xi"], split(modes[256:]), (1,))
    return cat([even + odd, even - odd], 0).reshape(32, 16, 128)


def stage_y_inverse(t, got):
    kind = got.dtype
    got = got.reshape(8, 4, 16, 128)
    tile = [got[:, i].reshape(128, 128).astype(F32) for i in range(4)]
    x = cat([f(tile[2 * a], tile[2 * a + 1]) for f in (low_halves, high_halves) for a in (0, 1)], 1)
    return [pair_swapped(nn(t["pi"][...], part).astype(BF), 128, 2) for part in parts_of(x, kind)]


def y_inverse_field(t, left, i):
    field = table_right(
        nn, [p[1 if i == 0 else 0] for p in left], t["yi" if i == 1 else "yt"]
    )
    tiles = transpose_groups(
        cat([field[16 * k : 16 * k + 16, 128 * h : 128 * h + 128] for h in (0, 1)], 0)
        for k in range(8)
    )
    return jnp.stack([tiles[k][16 * h : 16 * h + 16] for h in (0, 1) for k in range(8)], axis=0)


def z_inverse_field(t, got, i):
    m = parts_of(got.reshape(256, 128), got.dtype)
    return table_right(tn, m, t["zi"], (1 if i == 2 else 0,)).astype(BF)


def block_cells(psi):
    rows = []
    for par in (0, 1):
        for i in range(3):
            for a in (0, 1):
                rows.append(
                    cat(
                        [
                            psi[i][32 * x + 16 * a : 32 * x + 16 * a + 16, 128 * par : 128 * par + 128]
                            for x in range(4)
                        ],
                        1,
                    )
                )
    return cat(rows, 0)


def stage_z_backward(t, grad):
    out = []
    for i in range(3):
        block = []
        for x in range(4):
            for a in (0, 1):
                block.append(
                    cat(
                        [
                            grad[
                                16 * (6 * par + 2 * i + a) : 16 * (6 * par + 2 * i + a) + 16,
                                128 * x : 128 * x + 128,
                            ]
                            for par in (0, 1)
                        ],
                        1,
                    )
                )
        field = cat(block, 0)
        o = table_left(nt, t["zb"], split(field), (1 if i == 2 else 0,))
        out.append(o.reshape(16, 16, 128))
    return jnp.stack(out, axis=1)


def stage_y_backward(t, got):
    tiles = [
        cat([got[8 * h + i, f] for f in range(3) for h in (0, 1)], 0).astype(F32) for i in range(8)
    ]
    tiles = transpose_groups(tiles)
    x = cat(
        [
            cat([tiles[i][16 * (2 * f + h) : 16 * (2 * f + h) + 16] for i in range(8)], 0)
            for f in range(3)
            for h in (0, 1)
        ],
        1,
    )
    pairs = [
        pair_swapped(nn(t["pb"][...], part).astype(BF), 128, 3) for part in parts_of(x, got.dtype)
    ]
    gx = table_right(nn, [p[0] for p in pairs], t["yt"])
    rest = table_right(nn, [cat(p[1:], 1) for p in pairs], t["yb"])
    parts = []
    for a in (0, 1):
        u, v = gx[:, 128 * a : 128 * a + 128], rest[:, 128 * a : 128 * a + 128]
        parts += [low_halves(u, v), high_halves(u, v)]
    return jnp.stack([p.reshape(8, 16, 128) for p in parts], axis=1).reshape(32, 16, 128)


def stage_x_backward(t, got, inverse, along):
    planes = got.reshape(512, 128).astype(F32)
    low, high = planes[:256], planes[256:]
    even = table_left(nn, t["xb"], split(low + high), (0,))
    odd = table_left(nn, t["xb"], split(low - high), (1,))
    y = times_rows(cat([even, odd], 0), along)
    modes = times_rows(y + roll(y, 64), inverse)
    o = table_left(nn, t["xj"], split(modes))
    return jnp.where(lanes() < 64, o[:256], o[256:]).reshape(32, 8, 128)


def stage_y_final(t, got):
    kind = got.dtype
    got = got.reshape(8, 4, 8, 128)
    tile = [got[:, i].reshape(64, 128) for i in range(4)]
    x = cat([f(tile[2 * a], tile[2 * a + 1]) for f in (low_halves, high_halves) for a in (0, 1)], 1)
    lefts = [
        cat(pair_swapped(nn(t["pj"][...], part).astype(BF), 64, 2), 0)
        for part in parts_of(x, kind)
    ]
    out = table_right(nn, lefts, t["yt"])
    first, second = out[:64], out[64:]
    parts = []
    for a in (0, 1):
        u, v = first[:, 128 * a : 128 * a + 128], second[:, 128 * a : 128 * a + 128]
        parts += [low_halves(u, v), high_halves(u, v)]
    return cat([p.reshape(4, 16, 128) for p in parts], 0)


def stage_z_final(t, got):
    return table_right(tn, parts_of(got.reshape(256, 128), got.dtype), t["zj"])


def iota2(shape, dim):
    return lax.broadcasted_iota(jnp.int32, shape, dim)


def down_weights(t, wd):
    eight = nt(t["e1"][...], wd).astype(BF)
    row, col = iota2((384, 192), 0), iota2((384, 192), 1)
    w = jnp.where(row // 48 == (col % 16) // 2, nt(eight, t["e2t"][...]), 0.0).astype(BF)
    row, col = iota2((192, 384), 0), iota2((192, 384), 1)
    wt = jnp.where(col // 48 == (row % 16) // 2, nt(t["e2t"][...], eight), 0.0).astype(BF)
    return w, wt


def out_weights(t, wo):
    wide = wo.astype(F32)
    each = cat([jnp.broadcast_to(wide[j : j + 1], (8, 48)) for j in range(3)], 0).astype(BF)
    row, col = iota2((24, 384), 0), iota2((24, 384), 1)
    w = jnp.where(row % 8 == col // 48, nt(each, t["e1"][...]), 0.0).astype(BF)
    row, col = iota2((384, 24), 0), iota2((384, 24), 1)
    wt = jnp.where(row // 48 == col % 8, nt(t["e1"][...], each), 0.0).astype(BF)
    return w, wt


def bias_rows(t, b):
    out, left = 0.0, b
    for _ in range(3):
        part = left.astype(BF)
        out = out + nt(t["e1"][...], jnp.broadcast_to(part.astype(F32), (128, 48)).astype(BF))
        left = left - part.astype(F32)
    return out


def place(i):
    return (iota2((48, 432), 1) == 48 * i + iota2((48, 432), 0)).astype(F32).astype(BF)


def conv_weights(wc):
    out = 0.0
    for i in range(9):
        out = out + nn(cat([wc[9 * dx + i] for dx in range(3)], 0), place(i))
    return out.astype(BF)


def conv_weights_back(wc):
    rows = []
    for ex in range(3):
        out = 0.0
        for i in range(9):
            out = out + tn(wc[26 - 9 * ex - i], place(i))
        rows.append(out)
    return cat(rows, 0).astype(BF)


def add_taps(o):
    return o[:48, :512] + o[48:96, 128:640] + o[96:, 256:]


def add_own_taps(o):
    none = jnp.zeros((48, 128), F32)
    return o[48:96] + cat([none, o[:48, :384]], 1) + cat([o[96:, 128:], none], 1)


def gate(v):
    return 0.5 + 0.5 * jnp.tanh(0.5 * v)


TABLES = tables()
NAMES = tuple(TABLES)


Q_AHEAD = sorted(
    [(dz, dc) for dz in range(8) for dc in range(2) if dz or dc],
    key=lambda t: -(min(t[0], 8 - t[0]) + 0.3 * t[1]),
)
R_AHEAD = sorted(
    [(dx, dy) for dx in range(4) for dy in range(8) if dx or dy],
    key=lambda t: -(min(t[0], 4 - t[0]) + min(t[1], 8 - t[1])),
)
rem = lax.rem
div = lax.div


def kernel(*refs):
    args = refs[:8]
    count = len(NAMES)
    source = dict(zip(NAMES, refs[8 : 8 + count]))
    out = refs[8 + count]
    rest = refs[9 + count :]
    t = dict(zip(NAMES, rest[:count]))
    rest = rest[count:]
    here, rest = rest[:8], rest[8:]
    den, wd, bd, wc, bc, wo, obs, noi = here
    (s1, r1, s2, r2, s3, r3, s4, r4, s5, r5, s6, r6, s7, r7, s8, r8) = rest[:16]
    (fb, gb, sb, w1, w2, wb, wbt, wp, wpt, slope, pc, got_obs, got_noi, fac, bias) = rest[16:31]
    tsem, asem, ssem, rsem, hsem_s, hsem_r, osem_s, osem_r = rest[31:]

    s = lax.axis_index("slab")
    zh = lax.axis_index("pencil")
    core = rem(s, 2)
    r = rem(div(s, 2), 32)
    zl = div(s, 64)
    z = 2 * zh + zl
    q = 2 * z + core
    rx, ry = div(r, 8), rem(r, 8)

    def device(q, r):
        return {"slab": 64 * rem(div(q, 2), 2) + 2 * r + rem(q, 2), "pencil": div(q, 4)}

    def q_partners():
        for dz, dc in Q_AHEAD:
            z2 = rem(z + dz, 8) if dz else z
            c2 = 1 - core if dc else core
            yield (
                2 * z2 + c2,
                {"slab": 64 * rem(z2, 2) + 2 * r + c2, "pencil": div(z2, 2)},
            )

    def r_partners():
        for dx, dy in R_AHEAD:
            x2 = rem(rx + dx, 4) if dx else rx
            y2 = rem(ry + dy, 8) if dy else ry
            r2 = 8 * x2 + y2
            yield r2, {"slab": 64 * zl + 2 * r2 + core, "pencil": zh}

    first = NAMES.index("zf")

    def load(i):
        pltpu.make_async_copy(args[i], here[i], asem.at[i]).start()

    def load_table(i):
        pltpu.make_async_copy(source[NAMES[i]], t[NAMES[i]], tsem.at[i]).start()

    load(0)
    load_table(first)

    barrier = pltpu.get_barrier_semaphore()

    def greet(dev):
        pl.semaphore_signal(barrier, inc=1, device_id=dev, device_id_type=MESH)

    for _, dev in r_partners():
        greet(dev)
    for _, dev in q_partners():
        greet(dev)
    for dq in (1, 15):
        for dr in (1, 31):
            greet(device(rem(q + dq, 16), rem(r + dr, 32)))
    home = div(s, 4)
    slot = rem(s, 4)
    mine = home == r
    own = mine.astype(jnp.int32)
    for j in range(4):

        @pl.when(jnp.logical_not(mine & (rem(q, 4) == j)))
        def _():
            greet(device(4 * zh + j, home))

        @pl.when(jnp.logical_not(mine & (slot == j)))
        def _():
            greet({"slab": 4 * r + j, "pencil": zh})

    for i in (6, 7, *range(1, 6)):
        load(i)
    for i in range(len(NAMES)):
        if i != first:
            load_table(i)

    def ready(*names):
        for name in names:
            pltpu.make_async_copy(source[name], t[name], tsem.at[NAMES.index(name)]).wait()

    def have(*numbers):
        for i in numbers:
            pltpu.make_async_copy(args[i], here[i], asem.at[i]).wait()

    def send(phase, src, dst, me, partners):
        for d, dev in partners:
            pltpu.make_async_remote_copy(
                src_ref=src.at[d],
                dst_ref=dst.at[me],
                send_sem=ssem.at[phase],
                recv_sem=rsem.at[phase],
                device_id=dev,
                device_id_type=MESH,
            ).start()
        dst[me] = src[me]

    def send_q(phase, src, dst):
        send(phase, src, dst, q, q_partners())

    def send_r(phase, src, dst):
        send(phase, src, dst, r, r_partners())

    def arrived(phase, dst):
        part = dst.at[pl.ds(0, dst.shape[0] - 1)]
        pltpu.make_async_copy(part, part, rsem.at[phase]).wait()

    def sent(phase, src):
        part = src.at[pl.ds(0, src.shape[0] - 1)]
        pltpu.make_async_copy(part, part, ssem.at[phase]).wait()

    def halo(which, buf, action):
        cut = {0: ((1, 5), (1, 5)), 1: ((4, 5), (0, 1)), -1: ((1, 2), (5, 6))}
        line = {0: ((1, 9), (1, 9)), 1: ((8, 9), (0, 1)), -1: ((1, 2), (9, 10))}
        ways = ((1, 0), (-1, 0), (1, 1), (1, -1), (-1, 1), (-1, -1), (0, 1), (0, -1))
        for k, (dr, dq) in enumerate(ways):
            (a, b), (c, d) = cut[dr]
            (e, f), (g, h) = line[dq]
            copy = pltpu.make_async_remote_copy(
                src_ref=buf.at[pl.ds(a, b - a), pl.ds(e, f - e)],
                dst_ref=buf.at[pl.ds(c, d - c), pl.ds(g, h - g)],
                send_sem=hsem_s.at[which, k],
                recv_sem=hsem_r.at[which, k],
                device_id=device(rem(q + dq + 16, 16), rem(r + dr + 32, 32)),
                device_id_type=MESH,
            )
            action(copy)

    def shifted(buf, rows, tiles):
        lo, hi = rows
        for x in tiles:
            part = buf[x, lo:hi].reshape(48 * (hi - lo), 128)
            for dz, value in enumerate((roll(part, 1), part, roll(part, 127))):
                sb[lo:hi, 48 * dz : 48 * dz + 48, 128 * x : 128 * x + 128] = value.reshape(
                    hi - lo, 48, 128
                )

    def fill(buf, value):
        for x in range(4):
            buf[x + 1, 1:9] = value[:, 128 * x : 128 * x + 128].reshape(8, 48, 128)

    def conv(which, buf, weights):
        shifted(buf, (1, 9), range(1, 5))

        def inner(y, carry):
            o = nn(weights[...], sb[pl.ds(y, 3), :, 128:640].reshape(432, 512))
            pc[y] = add_own_taps(o)
            return carry

        lax.fori_loop(1, 7, inner, 0, unroll=2)
        halo(which, buf, lambda c: c.wait_recv())
        shifted(buf, (0, 10), (0, 5))
        shifted(buf, (0, 1), range(1, 5))
        shifted(buf, (9, 10), range(1, 5))

        def edges(y, carry):
            side = cat([sb[pl.ds(y, 3), :, 0:128], sb[pl.ds(y, 3), :, 640:768]], 2)
            o = nn(weights[...], side.reshape(432, 256))
            pc[y, :, 0:128] += o[:48, :128]
            pc[y, :, 384:512] += o[96:, 128:]
            return carry

        lax.fori_loop(1, 7, edges, 0, unroll=True)
        for y in (0, 7):
            pc[y] = add_taps(nn(weights[...], sb[y : y + 3].reshape(432, 768)))

    have(0)
    ready("zf")
    s1[...] = (stage_z_forward(t, den[...].reshape(128, 256))).astype(s1.dtype)
    have(6, 7)
    pl.semaphore_wait(barrier, 58 - 2 * own)
    send_q(0, s1, r1)

    def observed_copies(j, action):
        for src, dst, kind in (
            (obs.at[:, 0, pl.ds(8 * j, 8), :], got_obs.at[slot], 0),
            (noi.at[0, pl.ds(8 * j, 8), :], got_noi.at[slot], 1),
        ):
            action(
                pltpu.make_async_remote_copy(
                    src_ref=src,
                    dst_ref=dst,
                    send_sem=osem_s.at[kind, j],
                    recv_sem=osem_r.at[kind, slot],
                    device_id=device(4 * zh + j, home),
                    device_id_type=MESH,
                )
            )

    for j in range(4):
        this = mine & (rem(q, 4) == j)

        @pl.when(jnp.logical_not(this))
        def _():
            observed_copies(j, lambda c: c.start())

        @pl.when(this)
        def _():
            got_obs[slot] = obs[:, 0, 8 * j : 8 * j + 8, :]
            got_noi[slot] = noi[0, 8 * j : 8 * j + 8, :]

    inverse, both, along = factors(q, r)
    fac[0] = inverse
    fac[1] = both
    fac[2] = along
    ready("e1", "e2t")
    have(1, 2, 3, 4, 5)
    w, wt = down_weights(t, wd[...])
    wb[...] = w
    wbt[...] = wt
    w, wt = out_weights(t, wo[...])
    wp[...] = w
    wpt[...] = wt
    bias[0] = bias_rows(t, bd[...])
    bias[1] = bias_rows(t, bc[...])

    arrived(0, r1)
    ready("pf", "yt")
    s2[...] = (stage_y_forward(t, r1[...])).astype(s2.dtype)
    send_r(1, s2, r2)
    w1[...] = conv_weights(wc)
    arrived(1, r2)
    ready("xf", "xi")
    s3[...] = (stage_x_forward(t, r2[...], fac[1])).astype(s3.dtype)
    send_r(2, s3, r3)
    w2[...] = conv_weights_back(wc)
    arrived(2, r3)
    ready("pi", "yi")
    left = stage_y_inverse(t, r3[...])
    for i in range(3):
        s4[i] = y_inverse_field(t, left, i).astype(s4.dtype)
        send_q((3, 8, 9)[i], s4.at[i], r4.at[i])
    ready("zi", "zb", "pb", "yb", "xb", "xj", "pj", "zj")

    psi = []
    for i in range(3):
        arrived((3, 8, 9)[i], r4.at[i])
        psi.append(z_inverse_field(t, r4[i], i))
    cells = block_cells(psi)
    v = nn(wb[...], cells) + cat([bias[0]] * 4, 1)
    g = gate(v)
    fill(fb, (v * g).astype(BF))
    halo(0, fb, lambda c: c.start())
    slope[...] = g * (1.0 + v * (1.0 - g))
    conv(0, fb, w1)

    for j in range(4):

        @pl.when(jnp.logical_not(mine & (slot == j)))
        def _():
            pltpu.make_async_copy(got_obs.at[j], got_obs.at[j], osem_r.at[0, j]).wait()
            pltpu.make_async_copy(got_noi.at[j], got_noi.at[j], osem_r.at[1, j]).wait()

    v = pc[...].reshape(384, 512) + cat([bias[1]] * 4, 1)
    g = gate(v)
    hidden = (v * g).astype(BF)
    predicted = nn(wp[...], hidden)
    seen = cat([got_obs[x].reshape(24, 128) for x in range(4)], 1)
    weight = cat([cat([got_noi[x]] * 3, 0) for x in range(4)], 1)
    residual = weight * (predicted - seen)
    high, low = split(residual)
    back = nn(wpt[...], high) + nn(wpt[...], low)
    grad_conv = (back * (g * (1.0 + v * (1.0 - g)))).astype(BF)
    fill(gb, grad_conv)
    halo(1, gb, lambda c: c.start())
    conv(1, gb, w2)
    grad_down = (pc[...].reshape(384, 512) * slope[...]).astype(BF)
    s5[...] = (stage_z_backward(t, nn(wbt[...], grad_down))).astype(s5.dtype)

    send_q(4, s5, r5)
    arrived(4, r5)
    s6[...] = (stage_y_backward(t, r5[...])).astype(s6.dtype)
    send_r(5, s6, r6)
    arrived(5, r6)
    s7[...] = (stage_x_backward(t, r6[...], fac[0], fac[2])).astype(s7.dtype)
    send_r(6, s7, r7)
    arrived(6, r7)
    s8[...] = (stage_y_final(t, r7[...])).astype(s8.dtype)
    send_q(7, s8, r8)
    for phase, ref in zip((0, 1, 2, 4, 5, 6), (s1, s2, s3, s5, s6, s7)):
        sent(phase, ref)
    for i in range(3):
        sent((3, 8, 9)[i], s4.at[i])
    halo(0, fb, lambda c: c.wait_send())
    halo(1, gb, lambda c: c.wait_send())
    for j in range(4):

        @pl.when(jnp.logical_not(mine & (rem(q, 4) == j)))
        def _():
            observed_copies(j, lambda c: c.wait_send())

    arrived(7, r8)
    out[...] = stage_z_final(t, r8[...]).reshape(2, 64, 256)
    sent(7, s8)


def on_device(
    density, weight_down, bias_down, weight_conv, bias_conv, weight_out, observed, noise_precision
):
    vmem = pl.BlockSpec(memory_space=pltpu.VMEM)
    shapes = [(v.shape, BF) for v in TABLES.values()]
    inputs = (
        density,
        weight_down.T,
        bias_down.reshape(1, -1),
        weight_conv,
        bias_conv.reshape(1, -1),
        weight_out,
        observed,
        noise_precision,
    )
    shapes += [(v.shape, v.dtype) for v in inputs]
    wide, one = (16, 16, 128), (32, 8, 128)
    two, three, apart = (32, 16, 128), (16, 3, 16, 128), (3, 16, 16, 128)
    for shape, kind in zip((wide, one, two, apart, three, two, one, wide), KINDS):
        shapes += [(shape, kind)] * 2
    shapes += [
        ((6, 10, 48, 128), BF),
        ((6, 10, 48, 128), BF),
        ((10, 144, 768), BF),
        ((144, 432), BF),
        ((144, 432), BF),
        ((384, 192), BF),
        ((192, 384), BF),
        ((24, 384), BF),
        ((384, 24), BF),
        ((384, 512), F32),
        ((8, 48, 512), F32),
        ((4, 3, 8, 128), F32),
        ((4, 8, 128), F32),
        ((3, N, 128), F32),
        ((2, 384, 128), F32),
    ]
    dma = pltpu.SemaphoreType.DMA
    return pl.pallas_call(
        kernel,
        out_shape=jax.ShapeDtypeStruct((2, 64, 256), F32),
        in_specs=[pl.BlockSpec(memory_space=pltpu.HBM)] * (8 + len(NAMES)),
        out_specs=vmem,
        scratch_shapes=[pltpu.VMEM(shape, kind) for shape, kind in shapes]
        + [
            dma((len(NAMES),)),
            dma((8,)),
            dma((10,)),
            dma((10,)),
            dma((2, 8)),
            dma((2, 8)),
            dma((2, 4)),
            dma((2, 4)),
        ],
        compiler_params=pltpu.CompilerParams(
            collective_id=0, has_side_effects=True, vmem_limit_bytes=50 * 1024 * 1024
        ),
    )(
        *[pltpu.with_memory_space_constraint(v, pltpu.HBM) for v in inputs],
        *[pltpu.with_memory_space_constraint(jnp.asarray(TABLES[name]), pltpu.HBM) for name in NAMES],
    )


def solution(mesh):
    return jax.shard_map(
        on_device,
        mesh=mesh,
        in_specs=(
            P("slab", "pencil", None),
            P(),
            P(),
            P(),
            P(),
            P(),
            P(None, "slab", "pencil", None),
            P("slab", "pencil", None),
        ),
        out_specs=P("slab", "pencil", None),
        check_vma=False,
    )
```

```python
import functools

import jax
import jax.numpy as jnp
import ml_dtypes
import numpy as np
from jax import lax
from jax.experimental import pallas as pl
from jax.experimental.pallas import tpu as pltpu
from jax.sharding import PartitionSpec as P

MESH = pl.DeviceIdType.MESH
BF = jnp.bfloat16
F32 = jnp.float32
N = 256
GROWTH = 3.0
TWO_PI = 2.0 * np.pi
KINDS = (F32, F32, F32, F32, BF, F32, F32, F32)


def theta(a, b):
    return TWO_PI * ((a[:, None].astype(np.int64) * b[None, :]) % N) / N


def grid(*sizes):
    return [g.reshape(-1) for g in np.meshgrid(*[np.arange(s) for s in sizes], indexing="ij")]


def signed(k):
    return np.where(k < N // 2, k, k - N)


def wave(k):
    return np.where(k == N // 2, 0, signed(k)) * (TWO_PI / N)


def complex_rows(angle, c_out, c_in, sign, turn):
    value = np.exp(1j * sign * angle) * (1j**turn)
    a, b = c_out[:, None], c_in[None, :]
    same = a == b
    cross = np.where((a == 0) & (b == 1), -value.imag, value.imag)
    return np.where(same, value.real, cross)


def swap_rows(order_in, order_out, sign):
    rows_in = {key: i for i, key in enumerate(order_in)}
    count = len(order_in)
    out = np.zeros((2 * count, count))
    for i, key in enumerate(order_out):
        out[i, rows_in[key]] = 1.0
        name = dict(key)
        name["c"] = 1 - name["c"]
        other = tuple(name.items())
        out[count + i, rows_in[other]] = (1.0 if dict(key)["c"] == 0 else -1.0) * (-sign)
    return out


def keys(spec, canon):
    names = [n for n, _ in spec]
    axes = grid(*[s for _, s in spec])
    out = []
    for values in zip(*axes):
        d = dict(zip(names, (int(v) for v in values)))
        out.append(tuple((n, d[n]) for n in canon))
    return out


def tables():
    t = {}
    half = np.where(np.arange(N // 2) == 0, 1.0, 2.0) / float(N) ** 3
    z = np.arange(N)
    q, c, k = grid(16, 2, 8)
    kz = 8 * q + k
    t["zf"] = complex_rows(theta(kz, z), c, np.zeros(N, np.int64), -1, 0)
    par, zz = grid(2, 128)
    zc = 2 * zz + par
    back = complex_rows(theta(kz, zc), c, np.zeros(N, np.int64), -1, 0) * half[kz][:, None]
    t["zb"] = np.stack([back, back * wave(kz)[:, None]])
    q, k, c = grid(16, 8, 2)
    kz = 8 * q + k
    inv = complex_rows(theta(kz, zc).T, np.zeros(N, np.int64), c, 1, 0).T * half[kz][:, None]
    t["zi"] = np.stack([inv, inv * wave(kz)[:, None]])
    t["zj"] = complex_rows(theta(kz, z).T, np.zeros(N, np.int64), c, 1, 0).T
    a = np.arange(N)
    base = np.concatenate([np.cos(theta(a, a)), np.sin(theta(a, a))], axis=0)
    qy = wave(a)
    t["yt"] = base
    times = np.concatenate([qy, qy])[:, None] * base
    t["yi"] = times
    by = base * qy[None, :]
    t["yb"] = np.concatenate([by, base], axis=0)
    par, c_k, k2 = grid(2, 2, N // 2)
    kx = 2 * k2 + par
    r, w, c_in = grid(32, 4, 2)
    pos = lambda x1: 128 * (w // 2) + 4 * r + 2 * (w % 2) + x1
    t["xf"] = np.concatenate(
        [complex_rows(theta(kx, pos(v)), c_k, c_in, -1, 0) for v in (0, 1)], axis=0
    )
    t["xj"] = np.concatenate(
        [complex_rows(theta(kx, pos(v)).T, c_in, c_k, 1, -1) for v in (0, 1)], axis=0
    )
    c_h, k2 = grid(2, N // 2)
    r, c, x8 = grid(16, 2, 8)
    t["xi"] = np.stack(
        [complex_rows(theta(2 * k2 + p, 8 * r + x8).T, c, c_h, 1, 1) for p in (0, 1)]
    )
    r, x8, c = grid(16, 8, 2)
    t["xb"] = np.stack(
        [complex_rows(theta(2 * k2 + p, 8 * r + x8), c_h, c, -1, 0) for p in (0, 1)]
    )
    pairs = {}
    for name, value in t.items():
        high = value.astype(np.float32).astype(ml_dtypes.bfloat16)
        low = (value - high.astype(np.float64)).astype(np.float32).astype(ml_dtypes.bfloat16)
        pairs[name] = np.stack([high, low])
    canon = ("w", "c", "k")
    s = {}
    s["pf"] = swap_rows(
        keys((("w", 4), ("c", 2), ("k", 8)), canon), keys((("k", 8), ("w", 4), ("c", 2)), canon), -1
    )
    s["pj"] = swap_rows(
        keys((("k", 8), ("w", 4), ("c", 2)), canon), keys((("w", 4), ("k", 8), ("c", 2)), canon), 1
    )
    s["pi"] = swap_rows(
        keys((("k", 8), ("c", 2), ("w", 8)), canon), keys((("w", 8), ("k", 8), ("c", 2)), canon), 1
    )
    s["pb"] = swap_rows(
        keys((("w", 8), ("c", 2), ("k", 8)), canon), keys((("k", 8), ("w", 8), ("c", 2)), canon), -1
    )
    par, i, a, y = grid(2, 3, 2, 16)
    e2 = np.zeros((192, 24))
    e2[np.arange(192), 8 * i + 4 * a + 2 * (y % 2) + par] = 1.0
    s["e2t"] = e2
    e1 = np.zeros((384, 48))
    e1[np.arange(384), np.arange(384) % 48] = 1.0
    s["e1"] = e1
    for name, value in s.items():
        pairs[name] = value.astype(np.float32).astype(ml_dtypes.bfloat16)
    return pairs


def dot(a, b, ca, cb):
    return lax.dot_general(a, b, (((ca,), (cb,)), ((), ())), preferred_element_type=F32)


def nn(a, b):
    return dot(a, b, 1, 0)


def nt(a, b):
    return dot(a, b, 1, 1)


def tn(a, b):
    return dot(a, b, 0, 0)


def roll(x, shift):
    return pltpu.roll(x, shift % x.shape[-1], x.ndim - 1)


def split(x):
    high = x.astype(BF)
    return high, (x - high.astype(F32)).astype(BF)


def lanes():
    return lax.broadcasted_iota(jnp.int32, (1, 128), 1)


def low_halves(a, b):
    return jnp.where(lanes() < 64, a, roll(b, 64))


def high_halves(a, b):
    return jnp.where(lanes() < 64, roll(a, 64), b)


def transpose_groups(tiles):
    tiles = list(tiles)
    for d in (1, 2, 4):
        odd = (lanes() // (16 * d)) % 2 == 1
        for i in range(8):
            if i & d:
                continue
            low, high = tiles[i], tiles[i + d]
            tiles[i] = jnp.where(odd, roll(high, 16 * d), low)
            tiles[i + d] = jnp.where(odd, high, roll(low, 128 - 16 * d))
    return tiles


def cat(parts, axis):
    return jnp.concatenate(list(parts), axis=axis)


def parts_of(x, kind):
    return (x.astype(BF),) if kind == BF else split(x)


def pair_swapped(moved, rows, fields):
    return [
        cat([moved[:rows, 256 * f : 256 * f + 256], moved[rows:, 256 * f : 256 * f + 256]], 1)
        for f in range(fields)
    ]


def table_left(form, t, x, index=()):
    high, low = t[(0, *index)], t[(1, *index)]
    out = form(high, x[0]) + form(low, x[0])
    if len(x) > 1:
        out = out + form(high, x[1])
    return out


def table_right(form, x, t, index=()):
    high, low = t[(0, *index)], t[(1, *index)]
    out = form(x[0], high) + form(x[0], low)
    if len(x) > 1:
        out = out + form(x[1], high)
    return out


def stage_z_forward(t, density):
    return table_left(nt, t["zf"], split(density)).reshape(16, 16, 128)


def stage_y_forward(t, got):
    z_rows = [got[4 * i : 4 * i + 4].reshape(64, 128).astype(F32) for i in range(4)]
    x = cat(
        [f(z_rows[2 * a], z_rows[2 * a + 1]) for f in (low_halves, high_halves) for a in (0, 1)], 1
    )
    left = [
        cat(pair_swapped(nn(t["pf"][...], part).astype(BF), 64, 2), 0)
        for part in parts_of(x, got.dtype)
    ]
    out = table_right(nn, left, t["yt"])
    first, second = out[:64], out[64:]
    parts = []
    for a in (0, 1):
        u, v = first[:, 128 * a : 128 * a + 128], second[:, 128 * a : 128 * a + 128]
        parts += [low_halves(u, v), high_halves(u, v)]
    return jnp.stack([p.reshape(8, 8, 128) for p in parts], axis=1).reshape(32, 8, 128)


def factors(q, r):
    kz = 8 * q + r // 4
    row = lax.broadcasted_iota(jnp.int32, (N, 128), 0)
    lane = lax.broadcasted_iota(jnp.int32, (N, 128), 1)
    ky = 64 * (r % 4) + lane % 64
    spacing = F32(TWO_PI / N)

    kx = 2 * (row % 128) + row // 128

    def full(k):
        return jnp.where(k < N // 2, k, k - N).astype(F32) * spacing

    fx, fy = full(kx), full(ky)
    fz = (kz + 0 * row).astype(F32) * spacing
    square = fx * fx + fy * fy + fz * fz
    anchor = (kx == 0) & (ky == 0) & (kz == 0)
    square = jnp.where(anchor, F32(1.0), square)
    qx = jnp.where(kx == N // 2, F32(0.0), fx)
    first = lane < 64
    inverse = F32(GROWTH) / square
    return inverse, jnp.where(first, inverse, inverse * qx), jnp.where(first, qx, F32(1.0))


def times_rows(x, factor):
    half = N // 2
    return (x.reshape(2, 2, half, 128) * factor.reshape(2, 1, half, 128)).reshape(2 * N, 128)


def stage_x_forward(t, got, factor):
    y = table_left(nn, t["xf"], split(got.reshape(256, 128)))
    z = jnp.where(lanes() < 64, y[:512], y[512:])
    modes = times_rows(z + roll(z, 64), factor)
    even = table_left(nn, t["xi"], split(modes[:256]), (0,))
    odd = table_left(nn, t["xi"], split(modes[256:]), (1,))
    return cat([even + odd, even - odd], 0).reshape(32, 16, 128)


def stage_y_inverse(t, got):
    kind = got.dtype
    got = got.reshape(8, 4, 16, 128)
    tile = [got[:, i].reshape(128, 128).astype(F32) for i in range(4)]
    x = cat([f(tile[2 * a], tile[2 * a + 1]) for f in (low_halves, high_halves) for a in (0, 1)], 1)
    return [pair_swapped(nn(t["pi"][...], part).astype(BF), 128, 2) for part in parts_of(x, kind)]


def y_inverse_field(t, left, i):
    field = table_right(
        nn, [p[1 if i == 0 else 0] for p in left], t["yi" if i == 1 else "yt"]
    )
    tiles = transpose_groups(
        cat([field[16 * k : 16 * k + 16, 128 * h : 128 * h + 128] for h in (0, 1)], 0)
        for k in range(8)
    )
    return jnp.stack([tiles[k][16 * h : 16 * h + 16] for h in (0, 1) for k in range(8)], axis=0)


def z_inverse_field(t, got, i):
    m = parts_of(got.reshape(256, 128), got.dtype)
    return table_right(tn, m, t["zi"], (1 if i == 2 else 0,)).astype(BF)


def block_cells(psi):
    rows = []
    for par in (0, 1):
        for i in range(3):
            for a in (0, 1):
                rows.append(
                    cat(
                        [
                            psi[i][32 * x + 16 * a : 32 * x + 16 * a + 16, 128 * par : 128 * par + 128]
                            for x in range(4)
                        ],
                        1,
                    )
                )
    return cat(rows, 0)


def stage_z_backward(t, grad):
    out = []
    for i in range(3):
        block = []
        for x in range(4):
            for a in (0, 1):
                block.append(
                    cat(
                        [
                            grad[
                                16 * (6 * par + 2 * i + a) : 16 * (6 * par + 2 * i + a) + 16,
                                128 * x : 128 * x + 128,
                            ]
                            for par in (0, 1)
                        ],
                        1,
                    )
                )
        field = cat(block, 0)
        o = table_left(nt, t["zb"], split(field), (1 if i == 2 else 0,))
        out.append(o.reshape(16, 16, 128))
    return jnp.stack(out, axis=1)


def stage_y_backward(t, got):
    tiles = [
        cat([got[8 * h + i, f] for f in range(3) for h in (0, 1)], 0).astype(F32) for i in range(8)
    ]
    tiles = transpose_groups(tiles)
    x = cat(
        [
            cat([tiles[i][16 * (2 * f + h) : 16 * (2 * f + h) + 16] for i in range(8)], 0)
            for f in range(3)
            for h in (0, 1)
        ],
        1,
    )
    pairs = [
        pair_swapped(nn(t["pb"][...], part).astype(BF), 128, 3) for part in parts_of(x, got.dtype)
    ]
    gx = table_right(nn, [p[0] for p in pairs], t["yt"])
    rest = table_right(nn, [cat(p[1:], 1) for p in pairs], t["yb"])
    parts = []
    for a in (0, 1):
        u, v = gx[:, 128 * a : 128 * a + 128], rest[:, 128 * a : 128 * a + 128]
        parts += [low_halves(u, v), high_halves(u, v)]
    return jnp.stack([p.reshape(8, 16, 128) for p in parts], axis=1).reshape(32, 16, 128)


def stage_x_backward(t, got, inverse, along):
    planes = got.reshape(512, 128).astype(F32)
    low, high = planes[:256], planes[256:]
    even = table_left(nn, t["xb"], split(low + high), (0,))
    odd = table_left(nn, t["xb"], split(low - high), (1,))
    y = times_rows(cat([even, odd], 0), along)
    modes = times_rows(y + roll(y, 64), inverse)
    o = table_left(nn, t["xj"], split(modes))
    return jnp.where(lanes() < 64, o[:256], o[256:]).reshape(32, 8, 128)


def stage_y_final(t, got):
    kind = got.dtype
    got = got.reshape(8, 4, 8, 128)
    tile = [got[:, i].reshape(64, 128) for i in range(4)]
    x = cat([f(tile[2 * a], tile[2 * a + 1]) for f in (low_halves, high_halves) for a in (0, 1)], 1)
    lefts = [
        cat(pair_swapped(nn(t["pj"][...], part).astype(BF), 64, 2), 0)
        for part in parts_of(x, kind)
    ]
    out = table_right(nn, lefts, t["yt"])
    first, second = out[:64], out[64:]
    parts = []
    for a in (0, 1):
        u, v = first[:, 128 * a : 128 * a + 128], second[:, 128 * a : 128 * a + 128]
        parts += [low_halves(u, v), high_halves(u, v)]
    return cat([p.reshape(4, 16, 128) for p in parts], 0)


def stage_z_final(t, got):
    return table_right(tn, parts_of(got.reshape(256, 128), got.dtype), t["zj"])


def iota2(shape, dim):
    return lax.broadcasted_iota(jnp.int32, shape, dim)


def down_weights(t, wd):
    eight = nt(t["e1"][...], wd).astype(BF)
    row, col = iota2((384, 192), 0), iota2((384, 192), 1)
    w = jnp.where(row // 48 == (col % 16) // 2, nt(eight, t["e2t"][...]), 0.0).astype(BF)
    row, col = iota2((192, 384), 0), iota2((192, 384), 1)
    wt = jnp.where(col // 48 == (row % 16) // 2, nt(t["e2t"][...], eight), 0.0).astype(BF)
    return w, wt


def out_weights(t, wo):
    wide = wo.astype(F32)
    each = cat([jnp.broadcast_to(wide[j : j + 1], (8, 48)) for j in range(3)], 0).astype(BF)
    row, col = iota2((24, 384), 0), iota2((24, 384), 1)
    w = jnp.where(row % 8 == col // 48, nt(each, t["e1"][...]), 0.0).astype(BF)
    row, col = iota2((384, 24), 0), iota2((384, 24), 1)
    wt = jnp.where(row // 48 == col % 8, nt(t["e1"][...], each), 0.0).astype(BF)
    return w, wt


def bias_rows(t, b):
    out, left = 0.0, b
    for _ in range(3):
        part = left.astype(BF)
        out = out + nt(t["e1"][...], jnp.broadcast_to(part.astype(F32), (128, 48)).astype(BF))
        left = left - part.astype(F32)
    return out


def place(i):
    return (iota2((48, 432), 1) == 48 * i + iota2((48, 432), 0)).astype(F32).astype(BF)


def conv_weights(wc):
    out = 0.0
    for i in range(9):
        out = out + nn(cat([wc[9 * dx + i] for dx in range(3)], 0), place(i))
    return out.astype(BF)


def conv_weights_back(wc):
    rows = []
    for ex in range(3):
        out = 0.0
        for i in range(9):
            out = out + tn(wc[26 - 9 * ex - i], place(i))
        rows.append(out)
    return cat(rows, 0).astype(BF)


def add_taps(o):
    return o[:48, :512] + o[48:96, 128:640] + o[96:, 256:]


def add_own_taps(o):
    none = jnp.zeros((48, 128), F32)
    return o[48:96] + cat([none, o[:48, :384]], 1) + cat([o[96:, 128:], none], 1)


def gate(v):
    return 0.5 + 0.5 * jnp.tanh(0.5 * v)


TABLES = tables()
NAMES = tuple(TABLES)


Q_AHEAD = sorted(
    [(dz, dc) for dz in range(8) for dc in range(2) if dz or dc],
    key=lambda t: -(min(t[0], 8 - t[0]) + 0.3 * t[1]),
)
R_AHEAD = sorted(
    [(dx, dy) for dx in range(4) for dy in range(8) if dx or dy],
    key=lambda t: -(min(t[0], 4 - t[0]) + min(t[1], 8 - t[1])),
)
rem = lax.rem
div = lax.div


def kernel(*refs):
    args = refs[:8]
    count = len(NAMES)
    source = dict(zip(NAMES, refs[8 : 8 + count]))
    out = refs[8 + count]
    rest = refs[9 + count :]
    t = dict(zip(NAMES, rest[:count]))
    rest = rest[count:]
    here, rest = rest[:8], rest[8:]
    den, wd, bd, wc, bc, wo, obs, noi = here
    (s1, r1, s2, r2, s3, r3, s4, r4, s5, r5, s6, r6, s7, r7, s8, r8) = rest[:16]
    (fb, gb, sb, w1, w2, wb, wbt, wp, wpt, slope, pc, got_obs, got_noi, fac, bias) = rest[16:31]
    tsem, asem, ssem, rsem, hsem_s, hsem_r, osem_s, osem_r = rest[31:]

    s = lax.axis_index("slab")
    zh = lax.axis_index("pencil")
    core = rem(s, 2)
    r = rem(div(s, 2), 32)
    zl = div(s, 64)
    z = 2 * zh + zl
    q = 2 * z + core
    rx, ry = div(r, 8), rem(r, 8)

    def device(q, r):
        return {"slab": 64 * rem(div(q, 2), 2) + 2 * r + rem(q, 2), "pencil": div(q, 4)}

    def q_partners():
        for dz, dc in Q_AHEAD:
            z2 = rem(z + dz, 8) if dz else z
            c2 = 1 - core if dc else core
            yield (
                2 * z2 + c2,
                {"slab": 64 * rem(z2, 2) + 2 * r + c2, "pencil": div(z2, 2)},
            )

    def r_partners():
        for dx, dy in R_AHEAD:
            x2 = rem(rx + dx, 4) if dx else rx
            y2 = rem(ry + dy, 8) if dy else ry
            r2 = 8 * x2 + y2
            yield r2, {"slab": 64 * zl + 2 * r2 + core, "pencil": zh}

    first = NAMES.index("zf")

    def load(i):
        pltpu.make_async_copy(args[i], here[i], asem.at[i]).start()

    def load_table(i):
        pltpu.make_async_copy(source[NAMES[i]], t[NAMES[i]], tsem.at[i]).start()

    load(0)
    load_table(first)

    barrier = pltpu.get_barrier_semaphore()

    def greet(dev):
        pl.semaphore_signal(barrier, inc=1, device_id=dev, device_id_type=MESH)

    for _, dev in r_partners():
        greet(dev)
    for _, dev in q_partners():
        greet(dev)
    for dq in (1, 15):
        for dr in (1, 31):
            greet(device(rem(q + dq, 16), rem(r + dr, 32)))
    home = div(s, 4)
    slot = rem(s, 4)
    mine = home == r
    own = mine.astype(jnp.int32)
    for j in range(4):

        @pl.when(jnp.logical_not(mine & (rem(q, 4) == j)))
        def _():
            greet(device(4 * zh + j, home))

        @pl.when(jnp.logical_not(mine & (slot == j)))
        def _():
            greet({"slab": 4 * r + j, "pencil": zh})

    for i in (6, 7, *range(1, 6)):
        load(i)
    for i in range(len(NAMES)):
        if i != first:
            load_table(i)

    def ready(*names):
        for name in names:
            pltpu.make_async_copy(source[name], t[name], tsem.at[NAMES.index(name)]).wait()

    def have(*numbers):
        for i in numbers:
            pltpu.make_async_copy(args[i], here[i], asem.at[i]).wait()

    def send(phase, src, dst, me, partners):
        for d, dev in partners:
            pltpu.make_async_remote_copy(
                src_ref=src.at[d],
                dst_ref=dst.at[me],
                send_sem=ssem.at[phase],
                recv_sem=rsem.at[phase],
                device_id=dev,
                device_id_type=MESH,
            ).start()
        dst[me] = src[me]

    def send_q(phase, src, dst):
        send(phase, src, dst, q, q_partners())

    def send_r(phase, src, dst):
        send(phase, src, dst, r, r_partners())

    def arrived(phase, dst):
        part = dst.at[pl.ds(0, dst.shape[0] - 1)]
        pltpu.make_async_copy(part, part, rsem.at[phase]).wait()

    def sent(phase, src):
        part = src.at[pl.ds(0, src.shape[0] - 1)]
        pltpu.make_async_copy(part, part, ssem.at[phase]).wait()

    def halo(which, buf, action):
        cut = {0: ((1, 5), (1, 5)), 1: ((4, 5), (0, 1)), -1: ((1, 2), (5, 6))}
        line = {0: ((1, 9), (1, 9)), 1: ((8, 9), (0, 1)), -1: ((1, 2), (9, 10))}
        ways = ((1, 0), (-1, 0), (1, 1), (1, -1), (-1, 1), (-1, -1), (0, 1), (0, -1))
        for k, (dr, dq) in enumerate(ways):
            (a, b), (c, d) = cut[dr]
            (e, f), (g, h) = line[dq]
            copy = pltpu.make_async_remote_copy(
                src_ref=buf.at[pl.ds(a, b - a), pl.ds(e, f - e)],
                dst_ref=buf.at[pl.ds(c, d - c), pl.ds(g, h - g)],
                send_sem=hsem_s.at[which, k],
                recv_sem=hsem_r.at[which, k],
                device_id=device(rem(q + dq + 16, 16), rem(r + dr + 32, 32)),
                device_id_type=MESH,
            )
            action(copy)

    def shifted(buf, rows, tiles):
        lo, hi = rows
        for x in tiles:
            part = buf[x, lo:hi].reshape(48 * (hi - lo), 128)
            for dz, value in enumerate((roll(part, 1), part, roll(part, 127))):
                sb[lo:hi, 48 * dz : 48 * dz + 48, 128 * x : 128 * x + 128] = value.reshape(
                    hi - lo, 48, 128
                )

    def fill(buf, value):
        for x in range(4):
            buf[x + 1, 1:9] = value[:, 128 * x : 128 * x + 128].reshape(8, 48, 128)

    def conv(which, buf, weights):
        shifted(buf, (1, 9), range(1, 5))

        def inner(y, carry):
            o = nn(weights[...], sb[pl.ds(y, 3), :, 128:640].reshape(432, 512))
            pc[y] = add_own_taps(o)
            return carry

        lax.fori_loop(1, 7, inner, 0, unroll=True)
        halo(which, buf, lambda c: c.wait_recv())
        shifted(buf, (0, 10), (0, 5))
        shifted(buf, (0, 1), range(1, 5))
        shifted(buf, (9, 10), range(1, 5))

        def edges(y, carry):
            side = cat([sb[pl.ds(y, 3), :, 0:128], sb[pl.ds(y, 3), :, 640:768]], 2)
            o = nn(weights[...], side.reshape(432, 256))
            pc[y, :, 0:128] += o[:48, :128]
            pc[y, :, 384:512] += o[96:, 128:]
            return carry

        lax.fori_loop(1, 7, edges, 0, unroll=True)
        for y in (0, 7):
            pc[y] = add_taps(nn(weights[...], sb[y : y + 3].reshape(432, 768)))

    have(0)
    ready("zf")
    s1[...] = (stage_z_forward(t, den[...].reshape(128, 256))).astype(s1.dtype)
    have(6, 7)
    pl.semaphore_wait(barrier, 58 - 2 * own)
    send_q(0, s1, r1)

    def observed_copies(j, action):
        for src, dst, kind in (
            (obs.at[:, 0, pl.ds(8 * j, 8), :], got_obs.at[slot], 0),
            (noi.at[0, pl.ds(8 * j, 8), :], got_noi.at[slot], 1),
        ):
            action(
                pltpu.make_async_remote_copy(
                    src_ref=src,
                    dst_ref=dst,
                    send_sem=osem_s.at[kind, j],
                    recv_sem=osem_r.at[kind, slot],
                    device_id=device(4 * zh + j, home),
                    device_id_type=MESH,
                )
            )

    for j in range(4):
        this = mine & (rem(q, 4) == j)

        @pl.when(jnp.logical_not(this))
        def _():
            observed_copies(j, lambda c: c.start())

        @pl.when(this)
        def _():
            got_obs[slot] = obs[:, 0, 8 * j : 8 * j + 8, :]
            got_noi[slot] = noi[0, 8 * j : 8 * j + 8, :]

    inverse, both, along = factors(q, r)
    fac[0] = inverse
    fac[1] = both
    fac[2] = along
    ready("e1", "e2t")
    have(1, 2, 3, 4, 5)
    w, wt = down_weights(t, wd[...])
    wb[...] = w
    wbt[...] = wt
    w, wt = out_weights(t, wo[...])
    wp[...] = w
    wpt[...] = wt
    bias[0] = bias_rows(t, bd[...])
    bias[1] = bias_rows(t, bc[...])

    arrived(0, r1)
    ready("pf", "yt")
    s2[...] = (stage_y_forward(t, r1[...])).astype(s2.dtype)
    send_r(1, s2, r2)
    w1[...] = conv_weights(wc)
    arrived(1, r2)
    ready("xf", "xi")
    s3[...] = (stage_x_forward(t, r2[...], fac[1])).astype(s3.dtype)
    send_r(2, s3, r3)
    w2[...] = conv_weights_back(wc)
    arrived(2, r3)
    ready("pi", "yi")
    left = stage_y_inverse(t, r3[...])
    for i in range(3):
        s4[i] = y_inverse_field(t, left, i).astype(s4.dtype)
        send_q((3, 8, 9)[i], s4.at[i], r4.at[i])
    ready("zi", "zb", "pb", "yb", "xb", "xj", "pj", "zj")

    psi = []
    for i in range(3):
        arrived((3, 8, 9)[i], r4.at[i])
        psi.append(z_inverse_field(t, r4[i], i))
    cells = block_cells(psi)
    v = nn(wb[...], cells) + cat([bias[0]] * 4, 1)
    g = gate(v)
    fill(fb, (v * g).astype(BF))
    halo(0, fb, lambda c: c.start())
    slope[...] = g * (1.0 + v * (1.0 - g))
    conv(0, fb, w1)

    for j in range(4):

        @pl.when(jnp.logical_not(mine & (slot == j)))
        def _():
            pltpu.make_async_copy(got_obs.at[j], got_obs.at[j], osem_r.at[0, j]).wait()
            pltpu.make_async_copy(got_noi.at[j], got_noi.at[j], osem_r.at[1, j]).wait()

    v = pc[...].reshape(384, 512) + cat([bias[1]] * 4, 1)
    g = gate(v)
    hidden = (v * g).astype(BF)
    predicted = nn(wp[...], hidden)
    seen = cat([got_obs[x].reshape(24, 128) for x in range(4)], 1)
    weight = cat([cat([got_noi[x]] * 3, 0) for x in range(4)], 1)
    residual = weight * (predicted - seen)
    high, low = split(residual)
    back = nn(wpt[...], high) + nn(wpt[...], low)
    grad_conv = (back * (g * (1.0 + v * (1.0 - g)))).astype(BF)
    fill(gb, grad_conv)
    halo(1, gb, lambda c: c.start())
    conv(1, gb, w2)
    grad_down = (pc[...].reshape(384, 512) * slope[...]).astype(BF)
    s5[...] = (stage_z_backward(t, nn(wbt[...], grad_down))).astype(s5.dtype)

    send_q(4, s5, r5)
    arrived(4, r5)
    s6[...] = (stage_y_backward(t, r5[...])).astype(s6.dtype)
    send_r(5, s6, r6)
    arrived(5, r6)
    s7[...] = (stage_x_backward(t, r6[...], fac[0], fac[2])).astype(s7.dtype)
    send_r(6, s7, r7)
    arrived(6, r7)
    s8[...] = (stage_y_final(t, r7[...])).astype(s8.dtype)
    send_q(7, s8, r8)
    for phase, ref in zip((0, 1, 2, 4, 5, 6), (s1, s2, s3, s5, s6, s7)):
        sent(phase, ref)
    for i in range(3):
        sent((3, 8, 9)[i], s4.at[i])
    halo(0, fb, lambda c: c.wait_send())
    halo(1, gb, lambda c: c.wait_send())
    for j in range(4):

        @pl.when(jnp.logical_not(mine & (rem(q, 4) == j)))
        def _():
            observed_copies(j, lambda c: c.wait_send())

    arrived(7, r8)
    out[...] = stage_z_final(t, r8[...]).reshape(2, 64, 256)
    sent(7, s8)


def on_device(
    density, weight_down, bias_down, weight_conv, bias_conv, weight_out, observed, noise_precision
):
    vmem = pl.BlockSpec(memory_space=pltpu.VMEM)
    shapes = [(v.shape, BF) for v in TABLES.values()]
    inputs = (
        density,
        weight_down.T,
        bias_down.reshape(1, -1),
        weight_conv,
        bias_conv.reshape(1, -1),
        weight_out,
        observed,
        noise_precision,
    )
    shapes += [(v.shape, v.dtype) for v in inputs]
    wide, one = (16, 16, 128), (32, 8, 128)
    two, three, apart = (32, 16, 128), (16, 3, 16, 128), (3, 16, 16, 128)
    for shape, kind in zip((wide, one, two, apart, three, two, one, wide), KINDS):
        shapes += [(shape, kind)] * 2
    shapes += [
        ((6, 10, 48, 128), BF),
        ((6, 10, 48, 128), BF),
        ((10, 144, 768), BF),
        ((144, 432), BF),
        ((144, 432), BF),
        ((384, 192), BF),
        ((192, 384), BF),
        ((24, 384), BF),
        ((384, 24), BF),
        ((384, 512), F32),
        ((8, 48, 512), F32),
        ((4, 3, 8, 128), F32),
        ((4, 8, 128), F32),
        ((3, N, 128), F32),
        ((2, 384, 128), F32),
    ]
    dma = pltpu.SemaphoreType.DMA
    return pl.pallas_call(
        kernel,
        out_shape=jax.ShapeDtypeStruct((2, 64, 256), F32),
        in_specs=[pl.BlockSpec(memory_space=pltpu.HBM)] * (8 + len(NAMES)),
        out_specs=vmem,
        scratch_shapes=[pltpu.VMEM(shape, kind) for shape, kind in shapes]
        + [
            dma((len(NAMES),)),
            dma((8,)),
            dma((10,)),
            dma((10,)),
            dma((2, 8)),
            dma((2, 8)),
            dma((2, 4)),
            dma((2, 4)),
        ],
        compiler_params=pltpu.CompilerParams(
            collective_id=0, has_side_effects=True, vmem_limit_bytes=50 * 1024 * 1024
        ),
    )(
        *[pltpu.with_memory_space_constraint(v, pltpu.HBM) for v in inputs],
        *[pltpu.with_memory_space_constraint(jnp.asarray(TABLES[name]), pltpu.HBM) for name in NAMES],
    )


def solution(mesh):
    return jax.shard_map(
        on_device,
        mesh=mesh,
        in_specs=(
            P("slab", "pencil", None),
            P(),
            P(),
            P(),
            P(),
            P(),
            P(None, "slab", "pencil", None),
            P("slab", "pencil", None),
        ),
        out_specs=P("slab", "pencil", None),
        check_vma=False,
    )
```
